128 devices in a mesh: fsdp: 16 (over z_hi, x, core), ctx: 4 (over y), tp: 2 (over z_lo).
Axes of the slice: x: 4, y: 4, z: 4 (z_hi: 2, z_lo: 2; z = z_hi * 2 + z_lo), core: 2. Of those that a mesh axis runs over, the one named last changes fastest.
Arguments:
- tokens: bfloat16 [16, 512, 1024], P('fsdp', 'ctx'), may hold values from -6 to 6
- cotangent: bfloat16 [16, 512, 1024], P('fsdp', 'ctx'), may hold values from -6 to 6
- lengths: int32 [16], P('fsdp'), may hold values from 385 to 512, as said below
- expert_ids: int32 [16, 512, 8], P('fsdp', 'ctx'), may hold values from 0 to 15, all different within a row; in each aligned block of 128 rows (0 to 127, 128 to 255, ..., all dimensions but the last counted through in order) at most 96 rows name the same one
- router_gates: float32 [16, 512, 8], P('fsdp', 'ctx'), may hold values from 0.5 to 1.5
- attn_gain: bfloat16 [1024], P(('fsdp', 'ctx')), may hold values from 0.5 to 1.5
- ffn_gain: bfloat16 [1024], P(('fsdp', 'ctx')), may hold values from 0.5 to 1.5
- q_gain: bfloat16 [64], P(('fsdp', 'ctx')), may hold values from 0.5 to 1.5
- k_gain: bfloat16 [64], P(('fsdp', 'ctx')), may hold values from 0.5 to 1.5
- w_query: bfloat16 [1024, 16, 64], P(('fsdp', 'ctx'), 'tp'), may hold values from -0.1875 to 0.1875
- key_weight: bfloat16 [1024, 8, 64], P(('fsdp', 'ctx'), 'tp'), may hold values from -0.1875 to 0.1875
- value_weight: bfloat16 [1024, 8, 64], P(('fsdp', 'ctx'), 'tp'), may hold values from -0.1875 to 0.1875
- w_output: bfloat16 [1024, 16, 64], P(('fsdp', 'ctx'), 'tp'), may hold values from -0.75 to 0.75
- experts: bfloat16 [1024, 16, 3, 512], P(('fsdp', 'ctx'), None, None, 'tp'), may hold values from -0.1875 to 0.1875
Outputs:
- mixed: bfloat16 [16, 512, 1024], P('fsdp', 'ctx')
- tokens_grad: float32 [16, 512, 1024], P('fsdp', 'ctx')
- attn_gain_grad: float32 [1024], P(('fsdp', 'ctx'))
- ffn_gain_grad: float32 [1024], P(('fsdp', 'ctx'))
- q_gain_grad: float32 [64], P(('fsdp', 'ctx'))
- k_gain_grad: float32 [64], P(('fsdp', 'ctx'))
- w_query_grad: float32 [1024, 16, 64], P(('fsdp', 'ctx'), 'tp')
- w_key_grad: float32 [1024, 8, 64], P(('fsdp', 'ctx'), 'tp')
- w_value_grad: float32 [1024, 8, 64], P(('fsdp', 'ctx'), 'tp')
- w_output_grad: float32 [1024, 16, 64], P(('fsdp', 'ctx'), 'tp')
- experts_grad: float32 [1024, 16, 3, 512], P(('fsdp', 'ctx'), None, None, 'tp')
The draws below stay inside these ranges and needn't reach their ends.
Inputs may be any that keep to these rules, and one draw needn't show every extreme that they name: `lengths`: some slot has length 512. `expert_ids`: within the 128 rows of one slot on one index of ctx (aligned blocks), padding included, no expert is named by more than 96 rows, a bound that some block reaches. A row names 8 different experts.
All inputs are finite; a program needn't handle non-finite values.
Results may differ from the reference program's by a relative error of at most 0.025.
Values may be sent and summed in bfloat16 or wider, within the bound.
No kernel may reach another device: no remote copies, remote signals or barrier semaphores. Data moves between devices by JAX's collectives and lax.ppermute only.
A program may use at most 320 MiB of HBM per device.

```python
import math
import jax
import jax.numpy as jnp
import numpy as np
from jax import lax

MODEL_DIMENSION = 1024
QUERY_HEADS = 16
KEY_VALUE_HEADS = 8
HEAD_SIZE = 64
FF = 512
EXPERTS = 16
TOP = 8
SLOT_POSITIONS = 512
SLOTS = 16
ROWS = 128
CAP = 96
N_CTX = 4


def draw_lengths(key, part):
    key = jax.random.fold_in(key, 7)
    length_key, pick_key = jax.random.split(key)
    lengths_drawn = jax.random.randint(length_key, (SLOTS,), 3 * SLOT_POSITIONS // 4 + 1, SLOT_POSITIONS + 1)
    full_slot = jax.random.randint(pick_key, (), 0, SLOTS)
    return jnp.where(jnp.arange(SLOTS) == full_slot, SLOT_POSITIONS, lengths_drawn).astype(jnp.int32)


def block_scale(own_key, dims, cuts, least, top_value):
    def one(dim, blocks):
        heights = jax.random.uniform(jax.random.fold_in(jax.random.fold_in(own_key, 6), dim), (blocks,), jnp.float32, least / len(cuts), top_value / len(cuts))
        return jnp.repeat(jnp.exp(heights), dims[dim] // blocks).reshape((-1,) + (1,) * (len(dims) - dim - 1))

    gain = one(*cuts[0])
    for cut in cuts[1:]:
        gain = gain * one(*cut)
    return gain


def shared_out(stream_key, own, number, rows, number_of, top, reach, lean):
    ranking = jax.random.permutation(stream_key, number_of)
    packed, ordinary = load_shares(number_of, rows * top, reach, lean, True), load_shares(number_of, rows * top, reach, lean, False)
    places = jnp.arange(number_of)

    def named(sizes, offset_by):
        used = int((sizes > 0).sum())
        fixed = max(1, used // 4)
        moved = fixed + (places - fixed + offset_by * (used - fixed)) % max(1, number_of - fixed)
        return jnp.zeros((number_of,), jnp.int32).at[ranking[jnp.where(places < fixed, places, moved)]].set(jnp.asarray(sizes, jnp.int32))

    sizes = jnp.where(number % 4 == 0, named(packed, number // 4), named(ordinary, number - number // 4 - 1))
    mixed = jax.random.permutation(jax.random.fold_in(own, 3), number_of)
    source_of, sink = mixed[0:number_of // 2 * 2:2], mixed[1:number_of // 2 * 2:2]
    room = jnp.minimum(sizes[source_of] - 1, reach - sizes[sink]) // 2
    room = jnp.where((source_of == ranking[0]) | (sink == ranking[0]) | (sizes[sink] == 0), 0, jnp.maximum(room, 0))
    moved = jax.random.randint(jax.random.fold_in(own, 4), (number_of // 2,), 0, 1 << 20) % (room + 1)
    sizes = sizes.at[source_of].add(-moved).at[sink].add(moved)
    members = jnp.searchsorted(jnp.cumsum(sizes), jnp.arange(rows * top), side="right").astype(jnp.int32)
    listing = members.reshape(top, rows).T
    listing = listing[jax.random.permutation(jax.random.fold_in(own, 1), rows)]
    offset_by = jax.random.randint(jax.random.fold_in(own, 2), (rows, 1), 0, top)
    return jnp.take_along_axis(listing, (jnp.arange(top)[None, :] + offset_by) % top, axis=1)


def load_shares(number_of, total, reach, lean, full):
    weights = [(1 << 20) // math.isqrt(rank ** lean) + 1 for rank in range(1, number_of + 1)]
    largest = reach if full else min(reach, max(-(-total // number_of), total * weights[0] // sum(weights)))
    least = 1 if total - largest >= number_of - 1 else 0
    given, surplus = [largest] + [least] * (number_of - 1), total - largest - least * (number_of - 1)
    while surplus > 0:
        candidates = [i for i in range(1, number_of) if given[i] < largest] or [i for i in range(1, number_of) if given[i] < reach]
        mass, remaining = sum([weights[i] for i in candidates]), surplus
        for i in candidates:
            more = min(reach - given[i], max(1, remaining * weights[i] // mass), surplus)
            given[i] = given[i] + more
            surplus = surplus - more
    return np.array(given)


def gaussian(key, extent, spread, most, cuts=(), held_as=jnp.bfloat16):
    drawn = jax.random.normal(key, extent, jnp.float32) * spread
    if len(cuts) > 0:
        drawn = block_scale(key, extent, cuts, -0.22, 0.18) * drawn
    return jnp.clip(drawn, min=-most, max=most).astype(held_as)


def setup_inputs(seed: int = 0) -> dict:
    keys = jax.random.split(jax.random.key(seed), 15)
    tokens = gaussian(keys[0], (SLOTS, SLOT_POSITIONS, MODEL_DIMENSION), 1.0, 6.0, ((0, 16), (1, 4)))
    cotangent = gaussian(keys[1], (SLOTS, SLOT_POSITIONS, MODEL_DIMENSION), 1.0, 6.0, ((0, 16), (1, 4)))
    lengths = draw_lengths(jax.random.fold_in(keys[14], 71), 0)
    expert_ids_keys = jax.random.split(jax.random.fold_in(keys[3], 1), SLOTS * SLOT_POSITIONS // ROWS)
    expert_ids_turns = jax.random.permutation(jax.random.fold_in(keys[3], 3), SLOTS * SLOT_POSITIONS // ROWS)
    expert_ids = jax.vmap(lambda own, number: shared_out(jax.random.fold_in(keys[3], 2), own, number, ROWS, EXPERTS, TOP, CAP, 1))(expert_ids_keys, expert_ids_turns).reshape((SLOTS, SLOT_POSITIONS, TOP))
    router_gates = jnp.clip(0.5 + 1.0 * jax.random.uniform(keys[4], (SLOTS, SLOT_POSITIONS, TOP), jnp.float32) ** block_scale(keys[4], (SLOTS, SLOT_POSITIONS, TOP), ((0, 16), (1, 4)), -0.2, 0.2), 0.5, 1.5)
    attn_gain = jnp.clip(1.0 + 0.1 * jax.random.normal(keys[5], (MODEL_DIMENSION,), jnp.float32), 0.5, 1.5).astype(jnp.bfloat16)
    ffn_gain = jnp.clip(1.0 + 0.1 * jax.random.normal(keys[6], (MODEL_DIMENSION,), jnp.float32), 0.5, 1.5).astype(jnp.bfloat16)
    q_gain = jnp.clip(1.0 + 0.1 * jax.random.normal(keys[7], (HEAD_SIZE,), jnp.float32), 0.5, 1.5).astype(jnp.bfloat16)
    k_gain = jnp.clip(1.0 + 0.1 * jax.random.normal(keys[8], (HEAD_SIZE,), jnp.float32), 0.5, 1.5).astype(jnp.bfloat16)
    w_query = gaussian(keys[9], (MODEL_DIMENSION, QUERY_HEADS, HEAD_SIZE), MODEL_DIMENSION ** -0.5, 0.1875, ((0, 64), (1, 2)))
    key_weight = gaussian(keys[10], (MODEL_DIMENSION, KEY_VALUE_HEADS, HEAD_SIZE), MODEL_DIMENSION ** -0.5, 0.1875, ((0, 64), (1, 2)))
    value_weight = gaussian(keys[11], (MODEL_DIMENSION, KEY_VALUE_HEADS, HEAD_SIZE), MODEL_DIMENSION ** -0.5, 0.1875, ((0, 64), (1, 2)))
    w_output = gaussian(keys[12], (MODEL_DIMENSION, QUERY_HEADS, HEAD_SIZE), (QUERY_HEADS * HEAD_SIZE // 16) ** -0.5, 0.75, ((0, 64), (1, 2)))
    experts = gaussian(keys[13], (MODEL_DIMENSION, EXPERTS, 3, FF), MODEL_DIMENSION ** -0.5, 0.1875, ((0, 64), (3, 2)))
    return dict(tokens=tokens, cotangent=cotangent, lengths=lengths, expert_ids=expert_ids, router_gates=router_gates, attn_gain=attn_gain, ffn_gain=ffn_gain, q_gain=q_gain, k_gain=k_gain, w_query=w_query, key_weight=key_weight, value_weight=value_weight, w_output=w_output, experts=experts)


@jax.custom_vjp
def low(v):
    return lax.optimization_barrier(v.astype(jnp.bfloat16)).astype(jnp.float32)

@jax.custom_vjp
def low_back(v):
    return v

def low_keep(v):
    return (low(v), None)

def low_pass(kept, grad):
    return (grad,)

def back_keep(v):
    return (v, None)

def back_low(kept, grad):
    return (low(grad),)
low.defvjp(low_keep, low_pass)
low_back.defvjp(back_keep, back_low)
EPSILON = 1e-06
THETA_BASE = 1000000.0
NEG_FILL = -1e+30
HIGH = lax.Precision.HIGHEST

def inverse_rms(values):
    return lax.rsqrt(lax.optimization_barrier(jnp.mean(values * values, axis=-1, keepdims=True)) + EPSILON)

def rope_tables(positions, head_width):
    half_width = head_width // 2
    frequency = THETA_BASE ** (-(jnp.arange(half_width, dtype=jnp.float32) * 2.0) / head_width)
    angles = positions.astype(jnp.float32)[:, None] * frequency[None, :]
    return (jnp.cos(angles), jnp.sin(angles))

def rotate(values, cosine_table, sine_table):
    half_width = values.shape[-1] // 2
    first_half = values[..., :half_width]
    second_half = values[..., half_width:]
    cosine_part = cosine_table[:, None, :]
    sine_part = sine_table[:, None, :]
    return jnp.concatenate([first_half * cosine_part - second_half * sine_part, second_half * cosine_part + first_half * sine_part], axis=-1)

def route_slots(ids_flat, routes_valid, num_experts, capacity):
    onehot = ((ids_flat[:, None] == jnp.arange(num_experts, dtype=jnp.int32)[None, :]) & routes_valid[:, None]).astype(jnp.int32)
    route_rank = lax.optimization_barrier(jnp.sum(jnp.cumsum(onehot, axis=0) * onehot, axis=1)) - 1
    return jnp.where(routes_valid, ids_flat * capacity + route_rank, num_experts * capacity).astype(jnp.int32)

def attend_slot(slot_data):
    slot_of_query, key_slot, value_slot = slot_data
    grouped_heads = slot_of_query.reshape(SLOT_POSITIONS, KEY_VALUE_HEADS, QUERY_HEADS // KEY_VALUE_HEADS, HEAD_SIZE)
    raw_scores = low_back(jnp.einsum('rkgc,skc->kgrs', grouped_heads, key_slot, precision=HIGH) * HEAD_SIZE ** (-0.5))
    causal = jnp.arange(SLOT_POSITIONS)[None, :] <= jnp.arange(SLOT_POSITIONS)[:, None]
    probabilities = low(jax.nn.softmax(jnp.where(causal[None, None], raw_scores, NEG_FILL), axis=-1))
    heads_out = jnp.einsum('kgrs,skc->rkgc', probabilities, value_slot, precision=HIGH)
    return low_back(heads_out).reshape(SLOT_POSITIONS, QUERY_HEADS, HEAD_SIZE)

def expert_block(expert_mat, block_data):
    normed_rows, block_ids, block_gates, block_valid = block_data
    row_count = normed_rows.shape[0]
    routes_valid = jnp.repeat(block_valid, TOP) > 0.5
    route_slot = route_slots(block_ids.reshape(-1), routes_valid, EXPERTS, CAP)
    route_token = jnp.arange(row_count * TOP, dtype=jnp.int32) // TOP
    slot_token = jnp.zeros((EXPERTS * CAP + 1,), jnp.int32).at[route_slot].set(route_token)[:EXPERTS * CAP]
    picked = normed_rows[slot_token].reshape(EXPERTS, CAP, MODEL_DIMENSION)
    gate_up = jnp.einsum('ecd,dexf->ecxf', picked, expert_mat[:, :, 0:2], precision=HIGH)
    gate_pre = low_back(gate_up[:, :, 0])
    up_pre = low_back(gate_up[:, :, 1])
    expert_hidden = low(jax.nn.silu(gate_pre) * up_pre)
    outputs = low_back(jnp.einsum('ecf,def->ecd', expert_hidden, expert_mat[:, :, 2], precision=HIGH)).reshape(EXPERTS * CAP, MODEL_DIMENSION)
    padded = jnp.concatenate([outputs, jnp.zeros((1, MODEL_DIMENSION), outputs.dtype)], axis=0)
    per_route = padded[route_slot].reshape(row_count, TOP, MODEL_DIMENSION)
    return lax.optimization_barrier(jnp.sum(block_gates[:, :, None] * per_route, axis=1))

def reference(tokens, cotangent, lengths, expert_ids, router_gates, attn_gain, ffn_gain, q_gain, k_gain, w_query, key_weight, value_weight, w_output, experts):
    gate_values = router_gates.astype(jnp.float32)

    def forward(hidden_in, gain_one, gain_two, gain_query, gain_key, query_mat, key_mat, value_mat, output_mat, expert_mat):
        positions = jnp.arange(SLOT_POSITIONS, dtype=jnp.int32)
        valid_rows = (positions[None, :] < lengths[:, None]).astype(hidden_in.dtype)
        attn_input = low(hidden_in * inverse_rms(hidden_in) * gain_one)
        query_raw = low_back(jnp.einsum('tsd,dhc->tshc', attn_input, query_mat, precision=HIGH))
        key_raw = low_back(jnp.einsum('tsd,dhc->tshc', attn_input, key_mat, precision=HIGH))
        value_raw = low_back(jnp.einsum('tsd,dhc->tshc', attn_input, value_mat, precision=HIGH))
        cosine_table, sine_table = rope_tables(positions, HEAD_SIZE)
        query_low = low(rotate(query_raw * inverse_rms(query_raw) * gain_query, cosine_table, sine_table))
        key_low = low(rotate(key_raw * inverse_rms(key_raw) * gain_key, cosine_table, sine_table))
        value_low = low(value_raw)
        attn_heads = lax.map(jax.checkpoint(attend_slot), (query_low, key_low, value_low))
        attn_low = low(attn_heads)
        residual = hidden_in + low_back(jnp.einsum('tshc,dhc->tsd', attn_low, output_mat, precision=HIGH))
        ffn_input = low(residual * inverse_rms(residual) * gain_two)
        block_count = SLOTS * N_CTX
        blocks = (ffn_input.reshape(block_count, ROWS, MODEL_DIMENSION), expert_ids.reshape(block_count, ROWS, TOP), (gate_values * valid_rows[:, :, None]).reshape(block_count, ROWS, TOP), valid_rows.reshape(block_count, ROWS))
        run_block = jax.checkpoint(expert_block)
        expert_sum = lax.map(lambda block_data: run_block(expert_mat, block_data), blocks).reshape(SLOTS, SLOT_POSITIONS, MODEL_DIMENSION)
        return valid_rows[:, :, None] * (residual + expert_sum)
    floats = tuple((item.astype(jnp.float32) for item in (tokens, attn_gain, ffn_gain, q_gain, k_gain, w_query, key_weight, value_weight, w_output, experts)))
    result, pullback = jax.vjp(forward, *floats)
    gradients = pullback(cotangent.astype(jnp.float32))
    return (result.astype(jnp.bfloat16), gradients[0], gradients[1], gradients[2], gradients[3], gradients[4], gradients[5], gradients[6], gradients[7], gradients[8], gradients[9])
```

```python
import jax
import jax.numpy as jnp
import numpy as np
from jax import lax
from jax.experimental import pallas as pl
from jax.experimental.pallas import tpu as pltpu
from jax.sharding import Mesh, PartitionSpec as P

EPSILON = 1e-06
THETA_BASE = 1000000.0
NEG_FILL = -1e30
F32 = jnp.float32
BF16 = jnp.bfloat16
VMEM_LIMIT = 60 * 1024 * 1024
US = 1_100_000_000


def dot(a, b, ca=1, cb=0):
    return lax.dot_general(a, b, (((ca,), (cb,)), ((), ())), preferred_element_type=F32)


def inverse_rms(values):
    return lax.rsqrt(jnp.mean(values * values, axis=-1, keepdims=True) + EPSILON)


def norm_back(incoming, normed, inv_scale):
    return inv_scale * (incoming - normed * jnp.mean(incoming * normed, axis=-1, keepdims=True))


def rope_tables(seq, head_width):
    half = head_width // 2
    steps = np.tile(np.arange(half, dtype=np.float32), 4)
    frequency = np.float32(THETA_BASE) ** (-(steps * np.float32(2.0)) / np.float32(head_width))
    angles = np.arange(seq, dtype=np.float32)[:, None] * frequency[None, :]
    sign = np.where(np.arange(4 * half) % head_width < half, -1.0, 1.0).astype(np.float32)
    return jnp.asarray(np.cos(angles)), jnp.asarray(np.sin(angles) * sign)


def call(kernel, outs, *args, scratch=(), flops=0):
    smem = pl.BlockSpec(memory_space=pltpu.SMEM)
    vmem = pl.BlockSpec(memory_space=pltpu.VMEM)
    moved = sum(a.size * a.dtype.itemsize for a in args)
    moved += sum(o.size * o.dtype.itemsize for o in outs)
    return pl.pallas_call(
        kernel,
        out_shape=outs,
        in_specs=[smem if a.dtype == jnp.int32 and a.ndim == 1 else vmem for a in args],
        out_specs=[vmem] * len(outs),
        scratch_shapes=list(scratch),
        compiler_params=pltpu.CompilerParams(vmem_limit_bytes=VMEM_LIMIT),
        cost_estimate=pl.CostEstimate(flops=flops, bytes_accessed=moved, transcendentals=0),
    )(*args)


def shape(dims, dtype):
    return jax.ShapeDtypeStruct(dims, dtype)


def lanes(values):
    return lax.broadcasted_iota(jnp.int32, values.shape, len(values.shape) - 1)


def in_first(values):
    return lanes(values) < 64


def turned(values):
    return jnp.where(
        lanes(values) % 64 < 32, pltpu.roll(values, 96, 1), pltpu.roll(values, 32, 1)
    )


def doubled(values):
    return jnp.where(in_first(values), values, pltpu.roll(values, 64, 1))


def doubled_second(values):
    return jnp.where(in_first(values), pltpu.roll(values, 64, 1), values)


def head_mean(values):
    first = in_first(values)
    low = jnp.sum(jnp.where(first, values, 0.0), axis=1, keepdims=True)
    high = jnp.sum(jnp.where(first, 0.0, values), axis=1, keepdims=True)
    return jnp.where(first, low, high) * (1.0 / 64.0)


def head_only(values, g):
    keep = in_first(values) if g == 0 else lanes(values) >= 64
    return jnp.where(keep, values, jnp.zeros_like(values))


def head_gains(w_ref, n):
    column_q, column_k = w_ref[:, 258:259].astype(F32), w_ref[:, 259:260].astype(F32)
    row = lax.broadcasted_iota(jnp.int32, (w_ref.shape[0], 128), 0)
    lane = lanes(row) * n
    spread = jnp.where(row == lane, column_q, jnp.where(row == lane - 64 * n, column_k, 0.0))
    return jnp.sum(spread, axis=0, keepdims=True)


def row_of(w_ref, column):
    eye = lax.broadcasted_iota(jnp.int32, (128, 128), 0)
    eye = eye == lanes(eye)
    blocks = []
    for i in range(w_ref.shape[0] // 128):
        values = w_ref[i * 128 : (i + 1) * 128, column : column + 1].astype(F32)
        blocks.append(jnp.sum(jnp.where(eye, values, 0.0), axis=0, keepdims=True))
    return jnp.concatenate(blocks, axis=1)


def heads_of(raw, w_ref, n, cosine, sine):
    gains = head_gains(w_ref, n)
    gain_q, gain_k = doubled(gains), doubled_second(gains)
    q_raw, kv_raw = raw[:, :128], raw[:, 128:]
    q_inv = lax.rsqrt(head_mean(q_raw * q_raw) + EPSILON)
    k_inv = lax.rsqrt(head_mean(kv_raw * kv_raw) + EPSILON)
    q_hat, k_hat = q_raw * q_inv, kv_raw * k_inv
    q_turn, k_turn = q_hat * gain_q, k_hat * gain_k
    q = (q_turn * cosine + turned(q_turn) * sine).astype(BF16)
    k = (k_turn * cosine + turned(k_turn) * sine)
    k = doubled(k).astype(BF16)
    v = doubled_second(kv_raw).astype(BF16)
    return q, k, v, q_hat, k_hat, q_inv, k_inv, gain_q, gain_k


def probabilities(q, k, g, half):
    n = q.shape[0] // 2
    q, k = q[half * n : (half + 1) * n], k[: (half + 1) * n]
    scores = dot(head_only(q, g), k, 1, 1) * 0.125
    row = lax.broadcasted_iota(jnp.int32, scores.shape, 0) + half * n
    scores = jnp.where(lanes(scores) <= row, scores, NEG_FILL)
    exps = jnp.exp(scores - jnp.max(scores, axis=1, keepdims=True))
    return exps / jnp.sum(exps, axis=1, keepdims=True)


def column_of(ref):
    n = ref.shape[1]
    eye = lax.broadcasted_iota(jnp.int32, (n, n), 0)
    eye = eye == lanes(eye)
    return jnp.sum(jnp.where(eye, ref[...].astype(F32), 0.0), axis=1, keepdims=True)


def pack_kernel(wq, wk, wv, wo, one, two, qg, kg, m0, m1, m2, m3, held):
    n = wq.shape[0]
    lane = lax.broadcasted_iota(jnp.int32, (n, 128), 1)
    gains = jnp.where(lane == 0, column_of(one), jnp.where(lane == 1, column_of(two), 0.0))
    gains = jnp.where(lane == 2, qg[...].astype(F32), gains)
    gains = jnp.where(lane == 3, kg[...].astype(F32), gains).astype(BF16)
    q, k, v, o = (ref[...].astype(F32) for ref in (wq, wk, wv, wo))
    for j in range(4):
        held[j, :, 0:64] = q[:, 2 * j, :].astype(BF16)
        held[j, :, 64:128] = q[:, 2 * j + 1, :].astype(BF16)
        held[j, :, 128:192] = k[:, j, :].astype(BF16)
        held[j, :, 192:256] = v[:, j, :].astype(BF16)
        held[j, :, 256:384] = gains
    out = jnp.concatenate([o[:, i, :] for i in range(8)], axis=1).astype(BF16)
    at_y = lax.axis_index("y")
    for i, m in enumerate((m0, m1, m2, m3)):
        m[:, :384] = held[lax.rem(at_y + i, 4)]
        m[:, 384:] = out


def route_kernel(at, lengths, cot, ids, gates, copies):
    rows = cot.shape[0]
    row = lax.broadcasted_iota(jnp.int32, (rows, 1), 0) + at[0] * rows
    expert = lax.broadcasted_iota(jnp.int32, (rows, rows), 0)
    total = jnp.zeros((rows, rows), F32)
    for k in range(ids.shape[0]):
        total = total + jnp.where(ids[k : k + 1, :] == expert, gates[k : k + 1, :], 0.0)
    total = jnp.where(row < lengths[0], jnp.transpose(total), 0.0)
    high = total.astype(BF16).astype(F32)
    codes = (high + pltpu.roll(total - high, 16, 1)).astype(BF16)
    for i in range(copies.shape[0]):
        copies[i, :, :1024] = cot[...]
        copies[i, :, 1024:] = codes


def rows_in_order(at, arrived, out):
    n = arrived[0].shape[0] // 32
    for c, ref in enumerate(arrived):
        for i in range(32):
            y = lax.rem(at[0] + 4 - i % 4, 4)
            h = lax.rem(at[3] + i // 4 % 2, 2)
            x = lax.rem(at[4] + i // 8, 4)
            block = ((h * 4 + x) * 2 + lax.rem(at[1] + c, 2)) * 4 + y
            out[pl.ds(pl.multiple_of(block * n, n), n), :] = ref[i * n : (i + 1) * n, :]


def attend_kernel(
    at, tokens, wa, wb, cosine, sine, w, gains, into, raw, p0, p1, p2, p3, low
):
    n = wa.shape[0] // 32
    rows_in_order(at, (wa, wb), w)
    rows = p0.shape[0]
    gain_one = row_of(w, 256)
    gains[0:1, :] = gain_one
    gains[1:2, :] = row_of(w, 257)
    x = tokens[...].astype(F32)
    into[...] = (x * inverse_rms(x) * gain_one).astype(BF16)
    raw[...] = dot(into[...], w[:, :256])
    q, k, v = heads_of(raw[...], w, n, cosine[...], sine[...])[:3]
    n = q.shape[0] // 2
    for half in range(2):
        keys = slice(0, (half + 1) * n)
        out = [dot(probabilities(q, k, g, half).astype(BF16), v[keys]) for g in range(2)]
        low[half * n : (half + 1) * n, :] = jnp.where(in_first(out[0]), out[0], out[1]).astype(BF16)
    for k, part in enumerate((p0, p1, p2, p3)):
        start = pl.multiple_of(lax.rem(at[0] + k, 4) * rows, rows)
        part[...] = low[pl.ds(start, rows), :]


def spread_of(n):
    return 1.0 + lax.broadcasted_iota(jnp.int32, (n, 128), 0).astype(F32) * (1.0 / n)


def attend_back_kernel(
    at, g0, g1, g2, g3, into, raw, w, cosine, sine, og, a, dw0, dw1, p0, p1, p2, p3,
    grad, back, dw
):
    rows = g0.shape[0]
    for i, g in enumerate((g0, g1, g2, g3)):
        start = pl.multiple_of(lax.rem(at[0] + 4 - i, 4) * rows, rows)
        grad[pl.ds(start, rows), :] = g[...]
    n = dw0.shape[2]
    q, k, v, q_hat, k_hat, q_inv, k_inv, gain_q, gain_k = heads_of(
        raw[...], w, n, cosine[...], sine[...]
    )
    out_grad = grad[...]
    m = q.shape[0] // 2
    dq, dk, dv = [], [], []
    for half in range(2):
        rows_of, keys = slice(half * m, (half + 1) * m), slice(0, (half + 1) * m)
        dq_of, dk_of, dv_of = [], 0.0, 0.0
        for g in range(2):
            probs = probabilities(q, k, g, half)
            own = head_only(out_grad[rows_of], g)
            dv_of = dv_of + dot(probs.astype(BF16), own, 0, 0)
            probs_grad = dot(own, v[keys], 1, 1)
            delta = jnp.sum(probs * probs_grad, axis=1, keepdims=True)
            score_grad = (probs * (probs_grad - delta)).astype(BF16)
            dq_of.append(dot(score_grad, k[keys]))
            dk_of = dk_of + dot(score_grad, head_only(q[rows_of], g), 0, 0)
        dq.append(jnp.where(in_first(dq_of[0]), dq_of[0], dq_of[1]) * 0.125)
        dk.append(dk_of)
        dv.append(dv_of)
    dq = jnp.concatenate(dq, axis=0)
    dk = jnp.concatenate([dk[0] + dk[1][:m], dk[1][m:]], axis=0)
    dv = jnp.concatenate([dv[0] + dv[1][:m], dv[1][m:]], axis=0)
    dk = (dk + pltpu.roll(dk, 64, 1)) * 0.125
    dv = dv + pltpu.roll(dv, 64, 1)
    q_back = dq * cosine[...] - turned(dq) * sine[...]
    k_back = dk * cosine[...] - turned(dk) * sine[...]
    q_gain = jnp.sum(q_back * q_hat, axis=0, keepdims=True)
    k_gain = jnp.sum(k_back * k_hat, axis=0, keepdims=True)
    q_gain = q_gain + pltpu.roll(q_gain, 64, 1)
    k_gain = pltpu.roll(k_gain, 64, 1)
    q_scaled, k_scaled = q_back * gain_q, k_back * gain_k
    q_out = q_inv * (q_scaled - q_hat * head_mean(q_scaled * q_hat))
    k_out = k_inv * (k_scaled - k_hat * head_mean(k_scaled * k_hat))
    q_out = q_out.astype(BF16)
    kv_out = jnp.where(in_first(k_out), k_out, dv).astype(BF16)
    both = jnp.concatenate([q_out, kv_out], axis=1)
    back[...] = dot(both, w[:, :256], 1, 1).astype(BF16)
    for i, part in enumerate((p0, p1, p2, p3)):
        part[...] = back[pl.ds(pl.multiple_of(lax.rem(at[0] + i, 4) * rows, rows), rows), :]
    gains = (jnp.where(in_first(q_gain), q_gain, k_gain) * spread_of(n)).astype(BF16)
    dw[:, :256] = dot(into[...], both, 0, 0).astype(BF16)
    for i in range(64):
        dw[i * n : (i + 1) * n, 256:384] = gains
    dw[:, 384:] = dot(og[...], a[...], 0, 0).astype(BF16)
    for to in range(16):
        for h in range(2):
            block = (h * 4 + to // 4) * 8 + to % 4
            for r, out in enumerate((dw0, dw1)):
                start = pl.multiple_of((block + lax.rem(at[1] + r, 2) * 4) * n, n)
                out[to, h] = dw[pl.ds(start, n), :]


def project_kernel(at, p0, p1, p2, p3, wa, wb, a, part, w_out):
    rows_in_order(at, (wa, wb), w_out)
    total = 0.0
    for k, p in enumerate((p0, p1, p2, p3)):
        start = pl.multiple_of(lax.rem(at[0] + 4 - k, 4) * 128, 128)
        a[:, pl.ds(start, 128)] = p[...]
        total = total + dot(p[...], w_out[:, pl.ds(start, 128)], 1, 1)
    part[...] = total.astype(BF16)


def middle_kernel(mine, other, tokens, gains, resid, low):
    values = tokens[...].astype(F32) + (mine[...].astype(F32) + other[...].astype(F32))
    resid[...] = values
    low[...] = (values * inverse_rms(values) * gains[1:2, :]).astype(BF16)


def middle_back_kernel(
    at, lengths, mine, other, resid, cot, gains, w_out, resid_grad, low, p0, p1, p2, p3
):
    values = resid[...]
    row = lax.broadcasted_iota(jnp.int32, (values.shape[0], 1), 0) + at[0] * values.shape[0]
    upstream = jnp.where(row < lengths[0], cot[...].astype(F32), 0.0)
    inv = inverse_rms(values)
    incoming = (mine[...].astype(F32) + other[...].astype(F32)) * gains[1:2, :]
    total = upstream + norm_back(incoming, values * inv, inv)
    resid_grad[...] = total
    low[...] = total.astype(BF16)
    for k, p in enumerate((p0, p1, p2, p3)):
        start = pl.multiple_of(lax.rem(at[0] + k, 4) * 128, 128)
        p[...] = dot(low[...], w_out[:, pl.ds(start, 128)]).astype(BF16)


def first_back_kernel(mine, other, resid_grad, tokens, gains, out):
    x = tokens[...].astype(F32)
    inv = inverse_rms(x)
    incoming = (mine[...].astype(F32) + other[...].astype(F32)) * gains[0:1, :]
    out[...] = resid_grad[...] + norm_back(incoming, x * inv, inv)


def expert_kernel(at, f0, f1, f2, f3, u, wa, wb, p0, p1, p2, p3, grads, out, f, part):
    n = f0.shape[0]
    for k, block in enumerate((f0, f1, f2, f3)):
        f[pl.ds(pl.multiple_of(lax.rem(at[0] + k, 4) * n, n), n), :] = block[...]
    codes = u[:, 1024:].astype(F32)
    lane = lanes(codes)
    width = wa.shape[0]
    halves = [pl.ds(pl.multiple_of(lax.rem(at[3] + i, 2) * width, width), width) for i in range(2)]
    weights = list(zip((wa, wb), halves))
    for e in range(2):
        mine = (lane == at[2] + e) | (lane == at[2] + e + 16)
        gate = jnp.sum(jnp.where(mine, codes, 0.0), axis=1, keepdims=True)
        c = e * 768
        gate_up = sum(dot(f[:, d], w[:, c : c + 512]) for w, d in weights)
        hidden_grad = sum(dot(u[:, d], w[:, c + 512 : c + 768]) for w, d in weights) * gate
        gate_pre, up_pre = gate_up[:, :256], gate_up[:, 256:]
        sigma = jax.nn.sigmoid(gate_pre)
        activated = gate_pre * sigma
        slope = sigma + activated * (1.0 - sigma)
        grads[:, c : c + 256] = (hidden_grad * up_pre * slope).astype(BF16)
        grads[:, c + 256 : c + 512] = (hidden_grad * activated).astype(BF16)
        grads[:, c + 512 : c + 768] = (activated * up_pre * gate).astype(BF16)
    for w, d in weights:
        total = dot(grads[:, 0:512], w[:, 0:512], 1, 1)
        total = (total + dot(grads[:, 768:1280], w[:, 768:1280], 1, 1)).astype(BF16)
        part[:, d] = total
        total = dot(grads[:, 512:768], w[:, 512:768], 1, 1)
        total = total + dot(grads[:, 1280:1536], w[:, 1280:1536], 1, 1)
        out[:, d] = total.astype(BF16)
    for k, p in enumerate((p0, p1, p2, p3)):
        p[...] = part[pl.ds(pl.multiple_of(lax.rem(at[0] + k, 4) * n, n), n), :]


def expert_weights_kernel(at, *refs):
    blocks = (refs[0:4], refs[4:8])
    u0, u1, g0, g1, k0, s0, k1, s1, ft, ut, done = refs[8:]
    rows = u0.shape[0]
    n = k0.shape[4]
    for s, (f, u) in enumerate(zip(blocks, (u0, u1))):
        for k in range(4):
            start = pl.multiple_of(s * rows + lax.rem(at[0] + k, 4) * 128, 128)
            ft[:, pl.ds(start, 128)] = jnp.transpose(f[k][...])
        ut[:, s * rows : (s + 1) * rows] = jnp.transpose(u[:, :1024])

    def store(e, columns, into):
        keep, send = ((k0, s0), (k1, s1))[e]
        done[...] = into.astype(BF16)
        for i in range(64):
            r, h, y, c = i // 16, i // 8 % 2, i // 2 % 4, i % 2
            x = at[4] ^ ((0, 1, 3, 2), (0, 3, 1, 2))[e][r]
            h_to, c_to = lax.rem(at[3] + h, 2), lax.rem(at[1] + c, 2)
            y_to = lax.rem(at[0] + y, 4)
            start = pl.multiple_of((((h_to * 4 + x) * 2 + c_to) * 4 + y_to) * n, n)
            (keep if r < 2 else send)[r % 2, h, y, c, :, columns] = done[pl.ds(start, n), :]

    for e in range(2):

        @pl.loop(0, 2)
        def _(p, e=e):
            columns = pl.ds(pl.multiple_of(e * 768 + p * 256, 256), 256)
            into = dot(ft[:, :rows], g0[:, columns]) + dot(ft[:, rows:], g1[:, columns])
            store(e, pl.ds(pl.multiple_of(p * 256, 256), 256), into)

        columns = slice(e * 768 + 512, e * 768 + 768)
        down = dot(ut[:, :rows], g0[:, columns]) + dot(ut[:, rows:], g1[:, columns])
        store(e, slice(512, 768), down)


def owner_kernel(
    at, got, got_other, k0, k1, k2, k3, given, wq, wk, wv, we, one, two,
    dq, dk, dv, do, de, ends, held
):
    n = wq.shape[0]
    for c in range(2):
        for k, kept in enumerate((k0, k1, k2, k3)):
            y = lax.rem(at[0] + 4 - k, 4)
            first = (lax.rem(at[1] + c, 2) * 4 + y) * 2
            for e in range(2):
                held[first + e] = kept[e] if c == 0 else given[k, e]
    two_part = 0.0
    for x in range(3):
        for e in range(16):
            de[:, x, e, :] = held[e, :, x * 256 : (x + 1) * 256].astype(F32)
    for x in range(2):
        product = we[:, x].astype(F32) * de[:, x]
        two_part = two_part + jnp.sum(jnp.sum(product, axis=2), axis=1, keepdims=True)
    total = got[...].astype(F32) + got_other[...].astype(F32)
    block = lambda i: total[i * n : (i + 1) * n]
    rest = 0.0
    for j in range(4):
        for out, first, i in ((dq, 2 * j, j), (do, 2 * j, 12 + j)):
            out[:, first, :] = block(i)[:, 0:64]
            out[:, first + 1, :] = block(i)[:, 64:128]
        dk[:, j, :] = block(4 + j)[:, 0:64]
        dv[:, j, :] = block(4 + j)[:, 64:128]
        rest = rest + block(8 + j)
    one_part = 0.0
    for w, dw in ((wq, dq), (wk, dk), (wv, dv)):
        product = w[...].astype(F32) * dw[...]
        one_part = one_part + jnp.sum(jnp.sum(product, axis=2), axis=1, keepdims=True)
    gains = jnp.mean(rest / spread_of(n), axis=0, keepdims=True)
    row = lax.broadcasted_iota(jnp.int32, (n, 128), 0)
    lane = lanes(row)
    spread = jnp.where(lane == row, one_part / column_of(one), 0.0)
    spread = spread + jnp.where(lane == row + n, two_part / column_of(two), 0.0)
    ends[0:1, :] = jnp.sum(spread, axis=0, keepdims=True)
    ends[1:2, :] = gains


def swap(array, axis):
    return lax.ppermute(array, axis, [(0, 1), (1, 0)])


def from_ahead(array, axis, k):
    n = lax.axis_size(axis)
    return lax.ppermute(array, axis, [(i, (i - k) % n) for i in range(n)])


def to_ahead(array, axis, k):
    n = lax.axis_size(axis)
    return lax.ppermute(array, axis, [(i, (i + k) % n) for i in range(n)])


def ahead(axis, k):
    n = lax.axis_size(axis)
    return lax.rem(lax.axis_index(axis) + (k + n), n)


def after(value, *others):
    return lax.optimization_barrier((value, *others))[0]


def beside(array, odd):
    pairs = [(0, 3), (3, 0), (1, 2), (2, 1)] if odd else [(0, 1), (1, 0), (2, 3), (3, 2)]
    return lax.ppermute(array, "x", pairs)


def added(a, b):
    return (a.astype(F32) + b.astype(F32)).astype(BF16)


def relative(array, axis):
    return [array] + [from_ahead(array, axis, k) for k in range(1, lax.axis_size(axis))]


def sent_ahead(parts):
    return [to_ahead(p, "y", k) if k else p for k, p in enumerate(parts)]


def total_of(got):
    total = got[0].astype(F32)
    for g in got[1:]:
        total = total + g.astype(F32)
    return total.astype(BF16)


def local(
    tokens,
    cotangent,
    lengths,
    expert_ids,
    router_gates,
    attn_gain,
    ffn_gain,
    q_gain,
    k_gain,
    w_query,
    key_weight,
    value_weight,
    w_output,
    experts,
):
    rows, width = tokens.shape[1:]
    n_ctx = lax.axis_size("y")
    at_y, at_c = lax.axis_index("y"), lax.axis_index("c")
    at_h, at_x = lax.axis_index("h"), lax.axis_index("x")
    d_rows = w_query.shape[0]
    num_experts, _, ff = experts.shape[1:]
    held = num_experts // (n_ctx * 2)
    seq = rows * n_ctx
    apart = jnp.arange(4, dtype=jnp.int32) ^ at_x
    at = jnp.stack([at_y, at_c, (at_c * n_ctx + at_y) * held, at_h, at_x]).astype(jnp.int32)
    one_way = apart ^ (apart >> 1)
    other_way = (apart << 1) ^ ((apart >> 1) * 7)
    at = jnp.concatenate([at, one_way, other_way])
    cosine, sine = rope_tables(seq, w_query.shape[2])
    block = shape((rows, width), BF16)
    wide = shape((rows, width), F32)
    small = shape((rows, 128), BF16)

    messages = call(
        pack_kernel,
        [shape((d_rows, 896), BF16)] * 4,
        w_query,
        key_weight,
        value_weight,
        w_output,
        attn_gain[None],
        ffn_gain[None],
        q_gain[None],
        k_gain[None],
        scratch=[pltpu.VMEM((n_ctx, d_rows, 384), BF16)],
    )
    messages = sent_ahead(messages)
    w_near = jnp.concatenate([m[:, :384] for m in messages], axis=0)
    w_pair = jnp.concatenate([w_near, swap(w_near, "h")], axis=0)
    tokens_all = lax.all_gather(tokens[0], "y", axis=0, tiled=True)
    expert_rows = jnp.transpose(
        experts.reshape(d_rows, 2 * n_ctx, held, 3 * ff), (1, 0, 2, 3)
    ).reshape(2 * n_ctx, d_rows, held * 3 * ff)
    expert_rows = lax.all_to_all(after(expert_rows, w_near), ("c", "y"), 0, 0, tiled=True)
    expert_rows = expert_rows.reshape(2 * n_ctx * d_rows, held * 3 * ff)
    expert_other = swap(expert_rows, "h")
    expert_near = lax.all_gather(expert_rows, "x", axis=0, tiled=True)
    expert_far = lax.all_gather(expert_other, "x", axis=0, tiled=True)

    o_near = jnp.concatenate([m[:, 384:] for m in messages], axis=0)
    o_pair = jnp.concatenate([o_near, swap(o_near, "h")], axis=0)
    w_chunks = after(relative(w_pair, "x"), o_pair)
    w_own = jnp.concatenate(w_chunks, axis=0)
    u_own = call(
        route_kernel,
        [shape((n_ctx, rows, width + 128), BF16)],
        after(at, w_near),
        lengths,
        cotangent[0],
        expert_ids[0].T,
        router_gates[0].T,
        flops=2 * US,
    )[0]
    w_other = swap(after(w_own, tokens_all, expert_rows), "c")
    o_chunks = relative(after(o_pair, w_own), "x")

    weights, gains, into, raw, *parts = call(
        attend_kernel,
        [
            shape((width, 384), BF16),
            shape((2, width), F32),
            shape((seq, width), BF16),
            shape((seq, 256), F32),
            *[small] * 4,
        ],
        at,
        tokens_all,
        w_own,
        w_other,
        cosine,
        sine,
        scratch=[pltpu.VMEM((seq, 128), BF16)],
        flops=7 * US,
    )
    parts = sent_ahead(parts)
    o_own = jnp.concatenate(after(o_chunks, raw), axis=0)
    attn_low, mine, w_out = call(
        project_kernel,
        [shape((rows, 512), BF16), block, shape((width, 512), BF16)],
        after(at, expert_other),
        *parts,
        o_own,
        swap(o_own, "c"),
        flops=2 * US,
    )
    u_own = lax.all_to_all(after(u_own, attn_low), "y", 0, 0, tiled=True)
    u_own = u_own.reshape(seq, width + 128)
    resid, ffn_input = call(
        middle_kernel,
        [wide, block],
        mine,
        swap(mine, "l"),
        tokens[0],
        gains,
        flops=2 * US,
    )
    f_own = relative(ffn_input, "y")
    f_other = [swap(f, "c") for f in f_own]
    u_other = swap(after(u_own, *f_own), "c")

    def run_experts(f, u):
        return call(
            expert_kernel,
            [
                *[block] * 4,
                shape((seq, held * 3 * ff), BF16),
                shape((seq, width), BF16),
            ],
            at,
            *f,
            u,
            expert_near,
            expert_far,
            scratch=[pltpu.VMEM((seq, width), BF16)] * 2,
            flops=7 * US,
        )

    *part_other, g_other, out_other = run_experts(f_other, u_other)
    f_first = after(f_own, g_other)
    *part_own, g_own, out_own = run_experts(f_first, u_own)
    summed = [added(p, swap(q, "c")) for p, q in zip(part_own, part_other)]
    out_sum = added(out_own, swap(out_other, "c"))
    got = after(sent_ahead(summed), out_sum)
    mine = total_of(got)
    halves = shape((2, 2, n_ctx, 2, d_rows, 3 * ff), BF16)
    kept0, sent0, kept1, sent1 = call(
        expert_weights_kernel,
        [halves] * 4,
        after(at, summed),
        *f_own,
        *f_other,
        u_own,
        u_other,
        g_own,
        g_other,
        scratch=[
            pltpu.VMEM((width, 2 * seq), BF16),
            pltpu.VMEM((width, 2 * seq), BF16),
            pltpu.VMEM((width, 256), BF16),
        ],
        flops=10 * US,
    )
    resid_grad, out_grad, *attn_grads = call(
        middle_back_kernel,
        [wide, block, *[small] * 4],
        at,
        lengths,
        mine,
        swap(mine, "l"),
        resid,
        cotangent[0],
        gains,
        w_out,
        flops=3 * US,
    )
    attn_grads = sent_ahead(attn_grads)

    out_rows = lax.psum_scatter(after(out_sum, mine), "y", scatter_dimension=0, tiled=True)
    near = after([beside(sent0, True), beside(sent1, False)], attn_grads)
    kept = [added(kept0, near[0]), added(kept1, near[1])]
    far = [beside(k[1], e == 1) for e, k in enumerate(kept)]
    dw0, dw1, p0, p1, p2, p3 = call(
        attend_back_kernel,
        [shape((16, 2, d_rows, 896), BF16)] * 2 + [block] * 4,
        after(at, kept),
        *attn_grads,
        into,
        raw,
        weights,
        cosine,
        sine,
        out_grad,
        attn_low,
        scratch=[
            pltpu.VMEM((seq, 128), BF16),
            pltpu.VMEM((seq, width), BF16),
            pltpu.VMEM((width, 896), BF16),
        ],
        flops=US,
    )
    far = after(far, p0, out_rows)
    dw = added(dw0, swap(after(dw1, far), "c"))
    owned = lax.all_to_all(dw, ("x", "y"), 0, 0, tiled=True)
    owned = owned.reshape(4, n_ctx, 2, d_rows, 896).astype(F32)
    owned_into = jnp.sum(owned[..., :384], axis=0).reshape(n_ctx, 2, d_rows, 3, 128)
    owned_out = jnp.sum(owned[..., 384:], axis=(0, 1)).reshape(2, d_rows, 4, 128)
    owned = jnp.concatenate(
        [
            jnp.transpose(owned_into, (1, 3, 0, 2, 4)).reshape(2, -1, 128),
            jnp.transpose(owned_out, (0, 2, 1, 3)).reshape(2, -1, 128),
        ],
        axis=1,
    ).astype(BF16)
    owned_other = swap(lax.dynamic_index_in_dim(owned, 1 - at_h, 0, False), "h")
    owned = lax.dynamic_index_in_dim(owned, at_h, 0, False)
    mine = total_of(after(sent_ahead([p0, p1, p2, p3]), dw))
    tokens_grad = call(
        first_back_kernel,
        [wide],
        mine,
        swap(mine, "l"),
        resid_grad,
        tokens[0],
        gains,
        flops=2 * US,
    )[0]

    far = after(far, dw)
    sums = jnp.stack([added(k[0], f) for k, f in zip(kept, far)], axis=2)
    sums = added(sums[0], swap(sums[1], "h"))
    pieces = sent_ahead([sums[k] for k in range(n_ctx)])
    given = swap(jnp.stack([p[:, 1] for p in pieces]), "c")
    out_rows = added(out_rows, after(swap(out_rows, "l"), owned))
    *own_grads, expert_grads, ends = call(
        owner_kernel,
        [
            shape(w_query.shape, F32),
            shape(key_weight.shape, F32),
            shape(value_weight.shape, F32),
            shape(w_output.shape, F32),
            shape((d_rows, 3, num_experts, ff), F32),
            shape((2, 128), F32),
        ],
        after(at, out_rows),
        owned,
        owned_other,
        *[p[:, 0] for p in pieces],
        given,
        w_query,
        key_weight,
        value_weight,
        jnp.transpose(experts, (0, 2, 1, 3)),
        attn_gain[None],
        ffn_gain[None],
        scratch=[pltpu.VMEM((num_experts, d_rows, 3 * ff), BF16)],
        flops=4 * US,
    )
    positions = at_y * rows + jnp.arange(rows, dtype=jnp.int32)
    valid = (positions < lengths[0]).astype(F32)[:, None]
    mixed = (valid * (resid + out_rows.astype(F32))).astype(BF16)
    owner = ((at_h * 4 + at_x) * 2 + at_c) * n_ctx + at_y
    ends = ends + swap(ends, "l")
    pair = [lax.dynamic_slice(ends, (1, owner + k), (1, 1))[0] for k in (0, 64)]
    return (
        mixed[None],
        tokens_grad[None],
        ends[0, :d_rows],
        ends[0, d_rows : 2 * d_rows],
        *pair,
        *own_grads,
        jnp.transpose(expert_grads, (0, 2, 1, 3)),
    )


def solution(mesh):
    fine = Mesh(mesh.devices.reshape(2, 4, 2, 4, 2), ("h", "x", "c", "y", "l"))
    rows = P(("h", "x", "c"), "y", None)
    split = P(("h", "x", "c", "y"))
    heads = P(("h", "x", "c", "y"), "l", None)
    hidden = P(("h", "x", "c", "y"), None, None, "l")
    ins = (rows, rows, P(("h", "x", "c")), rows, rows)
    weights = (split, split, split, split, heads, heads, heads, heads, hidden)
    return jax.shard_map(
        local,
        mesh=fine,
        in_specs=ins + weights,
        out_specs=(rows, rows) + weights,
        check_vma=False,
    )
```

```python
import jax
import jax.numpy as jnp
import numpy as np
from jax import lax
from jax.experimental import pallas as pl
from jax.experimental.pallas import tpu as pltpu
from jax.sharding import Mesh, PartitionSpec as P

EPSILON = 1e-06
THETA_BASE = 1000000.0
NEG_FILL = -1e30
F32 = jnp.float32
BF16 = jnp.bfloat16
VMEM_LIMIT = 60 * 1024 * 1024
US = 1_100_000_000


def dot(a, b, ca=1, cb=0):
    return lax.dot_general(a, b, (((ca,), (cb,)), ((), ())), preferred_element_type=F32)


def inverse_rms(values):
    return lax.rsqrt(jnp.mean(values * values, axis=-1, keepdims=True) + EPSILON)


def norm_back(incoming, normed, inv_scale):
    return inv_scale * (incoming - normed * jnp.mean(incoming * normed, axis=-1, keepdims=True))


def rope_tables(seq, head_width):
    half = head_width // 2
    steps = np.tile(np.arange(half, dtype=np.float32), 4)
    frequency = np.float32(THETA_BASE) ** (-(steps * np.float32(2.0)) / np.float32(head_width))
    angles = np.arange(seq, dtype=np.float32)[:, None] * frequency[None, :]
    sign = np.where(np.arange(4 * half) % head_width < half, -1.0, 1.0).astype(np.float32)
    return jnp.asarray(np.cos(angles)), jnp.asarray(np.sin(angles) * sign)


def call(kernel, outs, *args, scratch=(), flops=0):
    smem = pl.BlockSpec(memory_space=pltpu.SMEM)
    vmem = pl.BlockSpec(memory_space=pltpu.VMEM)
    moved = sum(a.size * a.dtype.itemsize for a in args)
    moved += sum(o.size * o.dtype.itemsize for o in outs)
    return pl.pallas_call(
        kernel,
        out_shape=outs,
        in_specs=[smem if a.dtype == jnp.int32 and a.ndim == 1 else vmem for a in args],
        out_specs=[vmem] * len(outs),
        scratch_shapes=list(scratch),
        compiler_params=pltpu.CompilerParams(vmem_limit_bytes=VMEM_LIMIT),
        cost_estimate=pl.CostEstimate(flops=flops, bytes_accessed=moved, transcendentals=0),
    )(*args)


def shape(dims, dtype):
    return jax.ShapeDtypeStruct(dims, dtype)


def lanes(values):
    return lax.broadcasted_iota(jnp.int32, values.shape, len(values.shape) - 1)


def in_first(values):
    return lanes(values) < 64


def turned(values):
    return jnp.where(
        lanes(values) % 64 < 32, pltpu.roll(values, 96, 1), pltpu.roll(values, 32, 1)
    )


def doubled(values):
    return jnp.where(in_first(values), values, pltpu.roll(values, 64, 1))


def doubled_second(values):
    return jnp.where(in_first(values), pltpu.roll(values, 64, 1), values)


def head_mean(values):
    first = in_first(values)
    low = jnp.sum(jnp.where(first, values, 0.0), axis=1, keepdims=True)
    high = jnp.sum(jnp.where(first, 0.0, values), axis=1, keepdims=True)
    return jnp.where(first, low, high) * (1.0 / 64.0)


def head_only(values, g):
    keep = in_first(values) if g == 0 else lanes(values) >= 64
    return jnp.where(keep, values, jnp.zeros_like(values))


def head_gains(w_ref, n):
    column_q, column_k = w_ref[:, 258:259].astype(F32), w_ref[:, 259:260].astype(F32)
    row = lax.broadcasted_iota(jnp.int32, (w_ref.shape[0], 128), 0)
    lane = lanes(row) * n
    spread = jnp.where(row == lane, column_q, jnp.where(row == lane - 64 * n, column_k, 0.0))
    return jnp.sum(spread, axis=0, keepdims=True)


def row_of(w_ref, column):
    eye = lax.broadcasted_iota(jnp.int32, (128, 128), 0)
    eye = eye == lanes(eye)
    blocks = []
    for i in range(w_ref.shape[0] // 128):
        values = w_ref[i * 128 : (i + 1) * 128, column : column + 1].astype(F32)
        blocks.append(jnp.sum(jnp.where(eye, values, 0.0), axis=0, keepdims=True))
    return jnp.concatenate(blocks, axis=1)


def heads_of(raw, w_ref, n, cosine, sine):
    gains = head_gains(w_ref, n)
    gain_q, gain_k = doubled(gains), doubled_second(gains)
    q_raw, kv_raw = raw[:, :128], raw[:, 128:]
    q_inv = lax.rsqrt(head_mean(q_raw * q_raw) + EPSILON)
    k_inv = lax.rsqrt(head_mean(kv_raw * kv_raw) + EPSILON)
    q_hat, k_hat = q_raw * q_inv, kv_raw * k_inv
    q_turn, k_turn = q_hat * gain_q, k_hat * gain_k
    q = (q_turn * cosine + turned(q_turn) * sine).astype(BF16)
    k = (k_turn * cosine + turned(k_turn) * sine)
    k = doubled(k).astype(BF16)
    v = doubled_second(kv_raw).astype(BF16)
    return q, k, v, q_hat, k_hat, q_inv, k_inv, gain_q, gain_k


def probabilities(q, k, g, half):
    n = q.shape[0] // 2
    q, k = q[half * n : (half + 1) * n], k[: (half + 1) * n]
    scores = dot(head_only(q, g), k, 1, 1) * 0.125
    row = lax.broadcasted_iota(jnp.int32, scores.shape, 0) + half * n
    scores = jnp.where(lanes(scores) <= row, scores, NEG_FILL)
    exps = jnp.exp(scores - jnp.max(scores, axis=1, keepdims=True))
    return exps / jnp.sum(exps, axis=1, keepdims=True)


def column_of(ref):
    n = ref.shape[1]
    eye = lax.broadcasted_iota(jnp.int32, (n, n), 0)
    eye = eye == lanes(eye)
    return jnp.sum(jnp.where(eye, ref[...].astype(F32), 0.0), axis=1, keepdims=True)


def pack_kernel(wq, wk, wv, wo, one, two, qg, kg, m0, m1, m2, m3, held):
    n = wq.shape[0]
    lane = lax.broadcasted_iota(jnp.int32, (n, 128), 1)
    gains = jnp.where(lane == 0, column_of(one), jnp.where(lane == 1, column_of(two), 0.0))
    gains = jnp.where(lane == 2, qg[...].astype(F32), gains)
    gains = jnp.where(lane == 3, kg[...].astype(F32), gains).astype(BF16)
    q, k, v, o = (ref[...].astype(F32) for ref in (wq, wk, wv, wo))
    for j in range(4):
        held[j, :, 0:64] = q[:, 2 * j, :].astype(BF16)
        held[j, :, 64:128] = q[:, 2 * j + 1, :].astype(BF16)
        held[j, :, 128:192] = k[:, j, :].astype(BF16)
        held[j, :, 192:256] = v[:, j, :].astype(BF16)
        held[j, :, 256:384] = gains
    out = jnp.concatenate([o[:, i, :] for i in range(8)], axis=1).astype(BF16)
    at_y = lax.axis_index("y")
    for i, m in enumerate((m0, m1, m2, m3)):
        m[:, :384] = held[lax.rem(at_y + i, 4)]
        m[:, 384:] = out


def route_kernel(at, lengths, cot, ids, gates, copies):
    rows = cot.shape[0]
    row = lax.broadcasted_iota(jnp.int32, (rows, 1), 0) + at[0] * rows
    expert = lax.broadcasted_iota(jnp.int32, (rows, rows), 0)
    total = jnp.zeros((rows, rows), F32)
    for k in range(ids.shape[0]):
        total = total + jnp.where(ids[k : k + 1, :] == expert, gates[k : k + 1, :], 0.0)
    total = jnp.where(row < lengths[0], jnp.transpose(total), 0.0)
    high = total.astype(BF16).astype(F32)
    codes = (high + pltpu.roll(total - high, 16, 1)).astype(BF16)
    for i in range(copies.shape[0]):
        copies[i, :, :1024] = cot[...]
        copies[i, :, 1024:] = codes


def rows_in_order(at, arrived, out):
    n = arrived[0].shape[0] // 32
    for c, ref in enumerate(arrived):
        for i in range(32):
            y = lax.rem(at[0] + 4 - i % 4, 4)
            h = lax.rem(at[3] + i // 4 % 2, 2)
            x = lax.rem(at[4] + i // 8, 4)
            block = ((h * 4 + x) * 2 + lax.rem(at[1] + c, 2)) * 4 + y
            out[pl.ds(pl.multiple_of(block * n, n), n), :] = ref[i * n : (i + 1) * n, :]


def attend_kernel(
    at, tokens, wa, wb, cosine, sine, w, gains, into, raw, p0, p1, p2, p3, low
):
    n = wa.shape[0] // 32
    rows_in_order(at, (wa, wb), w)
    rows = p0.shape[0]
    gain_one = row_of(w, 256)
    gains[0:1, :] = gain_one
    gains[1:2, :] = row_of(w, 257)
    x = tokens[...].astype(F32)
    into[...] = (x * inverse_rms(x) * gain_one).astype(BF16)
    raw[...] = dot(into[...], w[:, :256])
    q, k, v = heads_of(raw[...], w, n, cosine[...], sine[...])[:3]
    n = q.shape[0] // 2
    for half in range(2):
        keys = slice(0, (half + 1) * n)
        out = [dot(probabilities(q, k, g, half).astype(BF16), v[keys]) for g in range(2)]
        low[half * n : (half + 1) * n, :] = jnp.where(in_first(out[0]), out[0], out[1]).astype(BF16)
    for k, part in enumerate((p0, p1, p2, p3)):
        start = pl.multiple_of(lax.rem(at[0] + k, 4) * rows, rows)
        part[...] = low[pl.ds(start, rows), :]


def spread_of(n):
    return 1.0 + lax.broadcasted_iota(jnp.int32, (n, 128), 0).astype(F32) * (1.0 / n)


def attend_back_kernel(
    at, g0, g1, g2, g3, into, raw, w, cosine, sine, og, a, dw0, dw1, p0, p1, p2, p3,
    grad, back, dw
):
    rows = g0.shape[0]
    for i, g in enumerate((g0, g1, g2, g3)):
        start = pl.multiple_of(lax.rem(at[0] + 4 - i, 4) * rows, rows)
        grad[pl.ds(start, rows), :] = g[...]
    n = dw0.shape[2]
    q, k, v, q_hat, k_hat, q_inv, k_inv, gain_q, gain_k = heads_of(
        raw[...], w, n, cosine[...], sine[...]
    )
    out_grad = grad[...]
    m = q.shape[0] // 2
    dq, dk, dv = [], [], []
    for half in range(2):
        rows_of, keys = slice(half * m, (half + 1) * m), slice(0, (half + 1) * m)
        dq_of, dk_of, dv_of = [], 0.0, 0.0
        for g in range(2):
            probs = probabilities(q, k, g, half)
            own = head_only(out_grad[rows_of], g)
            dv_of = dv_of + dot(probs.astype(BF16), own, 0, 0)
            probs_grad = dot(own, v[keys], 1, 1)
            delta = jnp.sum(probs * probs_grad, axis=1, keepdims=True)
            score_grad = (probs * (probs_grad - delta)).astype(BF16)
            dq_of.append(dot(score_grad, k[keys]))
            dk_of = dk_of + dot(score_grad, head_only(q[rows_of], g), 0, 0)
        dq.append(jnp.where(in_first(dq_of[0]), dq_of[0], dq_of[1]) * 0.125)
        dk.append(dk_of)
        dv.append(dv_of)
    dq = jnp.concatenate(dq, axis=0)
    dk = jnp.concatenate([dk[0] + dk[1][:m], dk[1][m:]], axis=0)
    dv = jnp.concatenate([dv[0] + dv[1][:m], dv[1][m:]], axis=0)
    dk = (dk + pltpu.roll(dk, 64, 1)) * 0.125
    dv = dv + pltpu.roll(dv, 64, 1)
    q_back = dq * cosine[...] - turned(dq) * sine[...]
    k_back = dk * cosine[...] - turned(dk) * sine[...]
    q_gain = jnp.sum(q_back * q_hat, axis=0, keepdims=True)
    k_gain = jnp.sum(k_back * k_hat, axis=0, keepdims=True)
    q_gain = q_gain + pltpu.roll(q_gain, 64, 1)
    k_gain = pltpu.roll(k_gain, 64, 1)
    q_scaled, k_scaled = q_back * gain_q, k_back * gain_k
    q_out = q_inv * (q_scaled - q_hat * head_mean(q_scaled * q_hat))
    k_out = k_inv * (k_scaled - k_hat * head_mean(k_scaled * k_hat))
    q_out = q_out.astype(BF16)
    kv_out = jnp.where(in_first(k_out), k_out, dv).astype(BF16)
    both = jnp.concatenate([q_out, kv_out], axis=1)
    back[...] = dot(both, w[:, :256], 1, 1).astype(BF16)
    for i, part in enumerate((p0, p1, p2, p3)):
        part[...] = back[pl.ds(pl.multiple_of(lax.rem(at[0] + i, 4) * rows, rows), rows), :]
    gains = (jnp.where(in_first(q_gain), q_gain, k_gain) * spread_of(n)).astype(BF16)
    dw[:, :256] = dot(into[...], both, 0, 0).astype(BF16)
    for i in range(64):
        dw[i * n : (i + 1) * n, 256:384] = gains
    dw[:, 384:] = dot(og[...], a[...], 0, 0).astype(BF16)
    for to in range(16):
        for h in range(2):
            block = (h * 4 + to // 4) * 8 + to % 4
            for r, out in enumerate((dw0, dw1)):
                start = pl.multiple_of((block + lax.rem(at[1] + r, 2) * 4) * n, n)
                out[to, h] = dw[pl.ds(start, n), :]


def project_kernel(at, p0, p1, p2, p3, wa, wb, a, part, w_out):
    rows_in_order(at, (wa, wb), w_out)
    total = 0.0
    for k, p in enumerate((p0, p1, p2, p3)):
        start = pl.multiple_of(lax.rem(at[0] + 4 - k, 4) * 128, 128)
        a[:, pl.ds(start, 128)] = p[...]
        total = total + dot(p[...], w_out[:, pl.ds(start, 128)], 1, 1)
    part[...] = total.astype(BF16)


def middle_kernel(mine, other, tokens, gains, resid, low):
    values = tokens[...].astype(F32) + (mine[...].astype(F32) + other[...].astype(F32))
    resid[...] = values
    low[...] = (values * inverse_rms(values) * gains[1:2, :]).astype(BF16)


def middle_back_kernel(
    at, lengths, mine, other, resid, cot, gains, w_out, resid_grad, low, p0, p1, p2, p3
):
    values = resid[...]
    row = lax.broadcasted_iota(jnp.int32, (values.shape[0], 1), 0) + at[0] * values.shape[0]
    upstream = jnp.where(row < lengths[0], cot[...].astype(F32), 0.0)
    inv = inverse_rms(values)
    incoming = (mine[...].astype(F32) + other[...].astype(F32)) * gains[1:2, :]
    total = upstream + norm_back(incoming, values * inv, inv)
    resid_grad[...] = total
    low[...] = total.astype(BF16)
    for k, p in enumerate((p0, p1, p2, p3)):
        start = pl.multiple_of(lax.rem(at[0] + k, 4) * 128, 128)
        p[...] = dot(low[...], w_out[:, pl.ds(start, 128)]).astype(BF16)


def first_back_kernel(mine, other, resid_grad, tokens, gains, out):
    x = tokens[...].astype(F32)
    inv = inverse_rms(x)
    incoming = (mine[...].astype(F32) + other[...].astype(F32)) * gains[0:1, :]
    out[...] = resid_grad[...] + norm_back(incoming, x * inv, inv)


def expert_kernel(at, f0, f1, f2, f3, u, wa, wb, p0, p1, p2, p3, grads, out, f, part):
    n = f0.shape[0]
    for k, block in enumerate((f0, f1, f2, f3)):
        f[pl.ds(pl.multiple_of(lax.rem(at[0] + k, 4) * n, n), n), :] = block[...]
    codes = u[:, 1024:].astype(F32)
    lane = lanes(codes)
    width = wa.shape[0]
    halves = [pl.ds(pl.multiple_of(lax.rem(at[3] + i, 2) * width, width), width) for i in range(2)]
    weights = list(zip((wa, wb), halves))
    for e in range(2):
        mine = (lane == at[2] + e) | (lane == at[2] + e + 16)
        gate = jnp.sum(jnp.where(mine, codes, 0.0), axis=1, keepdims=True)
        c = e * 768
        gate_up = sum(dot(f[:, d], w[:, c : c + 512]) for w, d in weights)
        hidden_grad = sum(dot(u[:, d], w[:, c + 512 : c + 768]) for w, d in weights) * gate
        gate_pre, up_pre = gate_up[:, :256], gate_up[:, 256:]
        sigma = jax.nn.sigmoid(gate_pre)
        activated = gate_pre * sigma
        slope = sigma + activated * (1.0 - sigma)
        grads[:, c : c + 256] = (hidden_grad * up_pre * slope).astype(BF16)
        grads[:, c + 256 : c + 512] = (hidden_grad * activated).astype(BF16)
        grads[:, c + 512 : c + 768] = (activated * up_pre * gate).astype(BF16)
    for w, d in weights:
        total = dot(grads[:, 0:512], w[:, 0:512], 1, 1)
        total = (total + dot(grads[:, 768:1280], w[:, 768:1280], 1, 1)).astype(BF16)
        part[:, d] = total
        total = dot(grads[:, 512:768], w[:, 512:768], 1, 1)
        total = total + dot(grads[:, 1280:1536], w[:, 1280:1536], 1, 1)
        out[:, d] = total.astype(BF16)
    for k, p in enumerate((p0, p1, p2, p3)):
        p[...] = part[pl.ds(pl.multiple_of(lax.rem(at[0] + k, 4) * n, n), n), :]


def expert_weights_kernel(at, *refs):
    blocks = (refs[0:4], refs[4:8])
    u0, u1, g0, g1, k0, s0, k1, s1, ft, ut, done = refs[8:]
    rows = u0.shape[0]
    n = k0.shape[4]
    for s, (f, u) in enumerate(zip(blocks, (u0, u1))):
        for k in range(4):
            start = pl.multiple_of(s * rows + lax.rem(at[0] + k, 4) * 128, 128)
            ft[:, pl.ds(start, 128)] = jnp.transpose(f[k][...])
        ut[:, s * rows : (s + 1) * rows] = jnp.transpose(u[:, :1024])

    def store(e, columns, into):
        keep, send = ((k0, s0), (k1, s1))[e]
        done[...] = into.astype(BF16)
        for i in range(64):
            r, h, y, c = i // 16, i // 8 % 2, i // 2 % 4, i % 2
            x = at[4] ^ ((0, 1, 3, 2), (0, 3, 1, 2))[e][r]
            h_to, c_to = lax.rem(at[3] + h, 2), lax.rem(at[1] + c, 2)
            y_to = lax.rem(at[0] + y, 4)
            start = pl.multiple_of((((h_to * 4 + x) * 2 + c_to) * 4 + y_to) * n, n)
            (keep if r < 2 else send)[r % 2, h, y, c, :, columns] = done[pl.ds(start, n), :]

    for e in range(2):

        @pl.loop(0, 2)
        def _(p, e=e):
            columns = pl.ds(pl.multiple_of(e * 768 + p * 256, 256), 256)
            into = dot(ft[:, :rows], g0[:, columns]) + dot(ft[:, rows:], g1[:, columns])
            store(e, pl.ds(pl.multiple_of(p * 256, 256), 256), into)

        columns = slice(e * 768 + 512, e * 768 + 768)
        down = dot(ut[:, :rows], g0[:, columns]) + dot(ut[:, rows:], g1[:, columns])
        store(e, slice(512, 768), down)


def owner_kernel(
    at, got, got_other, k0, k1, k2, k3, given, wq, wk, wv, we, one, two,
    dq, dk, dv, do, de, ends, held
):
    n = wq.shape[0]
    for c in range(2):
        for k, kept in enumerate((k0, k1, k2, k3)):
            y = lax.rem(at[0] + 4 - k, 4)
            first = (lax.rem(at[1] + c, 2) * 4 + y) * 2
            for e in range(2):
                held[first + e] = kept[e] if c == 0 else given[k, e]
    two_part = 0.0
    for x in range(3):
        for e in range(16):
            de[:, x, e, :] = held[e, :, x * 256 : (x + 1) * 256].astype(F32)
    for x in range(2):
        product = we[:, x].astype(F32) * de[:, x]
        two_part = two_part + jnp.sum(jnp.sum(product, axis=2), axis=1, keepdims=True)
    total = got[...].astype(F32) + got_other[...].astype(F32)
    block = lambda i: total[i * n : (i + 1) * n]
    rest = 0.0
    for j in range(4):
        for out, first, i in ((dq, 2 * j, j), (do, 2 * j, 12 + j)):
            out[:, first, :] = block(i)[:, 0:64]
            out[:, first + 1, :] = block(i)[:, 64:128]
        dk[:, j, :] = block(4 + j)[:, 0:64]
        dv[:, j, :] = block(4 + j)[:, 64:128]
        rest = rest + block(8 + j)
    one_part = 0.0
    for w, dw in ((wq, dq), (wk, dk), (wv, dv)):
        product = w[...].astype(F32) * dw[...]
        one_part = one_part + jnp.sum(jnp.sum(product, axis=2), axis=1, keepdims=True)
    gains = jnp.mean(rest / spread_of(n), axis=0, keepdims=True)
    row = lax.broadcasted_iota(jnp.int32, (n, 128), 0)
    lane = lanes(row)
    spread = jnp.where(lane == row, one_part / column_of(one), 0.0)
    spread = spread + jnp.where(lane == row + n, two_part / column_of(two), 0.0)
    ends[0:1, :] = jnp.sum(spread, axis=0, keepdims=True)
    ends[1:2, :] = gains


def swap(array, axis):
    return lax.ppermute(array, axis, [(0, 1), (1, 0)])


def from_ahead(array, axis, k):
    n = lax.axis_size(axis)
    return lax.ppermute(array, axis, [(i, (i - k) % n) for i in range(n)])


def to_ahead(array, axis, k):
    n = lax.axis_size(axis)
    return lax.ppermute(array, axis, [(i, (i + k) % n) for i in range(n)])


def ahead(axis, k):
    n = lax.axis_size(axis)
    return lax.rem(lax.axis_index(axis) + (k + n), n)


def after(value, *others):
    return lax.optimization_barrier((value, *others))[0]


def beside(array, odd):
    pairs = [(0, 3), (3, 0), (1, 2), (2, 1)] if odd else [(0, 1), (1, 0), (2, 3), (3, 2)]
    return lax.ppermute(array, "x", pairs)


def added(a, b):
    return (a.astype(F32) + b.astype(F32)).astype(BF16)


def relative(array, axis):
    return [array] + [from_ahead(array, axis, k) for k in range(1, lax.axis_size(axis))]


def sent_ahead(parts):
    return [to_ahead(p, "y", k) if k else p for k, p in enumerate(parts)]


def total_of(got):
    total = got[0].astype(F32)
    for g in got[1:]:
        total = total + g.astype(F32)
    return total.astype(BF16)


def local(
    tokens,
    cotangent,
    lengths,
    expert_ids,
    router_gates,
    attn_gain,
    ffn_gain,
    q_gain,
    k_gain,
    w_query,
    key_weight,
    value_weight,
    w_output,
    experts,
):
    rows, width = tokens.shape[1:]
    n_ctx = lax.axis_size("y")
    at_y, at_c = lax.axis_index("y"), lax.axis_index("c")
    at_h, at_x = lax.axis_index("h"), lax.axis_index("x")
    d_rows = w_query.shape[0]
    num_experts, _, ff = experts.shape[1:]
    held = num_experts // (n_ctx * 2)
    seq = rows * n_ctx
    apart = jnp.arange(4, dtype=jnp.int32) ^ at_x
    at = jnp.stack([at_y, at_c, (at_c * n_ctx + at_y) * held, at_h, at_x]).astype(jnp.int32)
    one_way = apart ^ (apart >> 1)
    other_way = (apart << 1) ^ ((apart >> 1) * 7)
    at = jnp.concatenate([at, one_way, other_way])
    cosine, sine = rope_tables(seq, w_query.shape[2])
    block = shape((rows, width), BF16)
    wide = shape((rows, width), F32)
    small = shape((rows, 128), BF16)

    messages = call(
        pack_kernel,
        [shape((d_rows, 896), BF16)] * 4,
        w_query,
        key_weight,
        value_weight,
        w_output,
        attn_gain[None],
        ffn_gain[None],
        q_gain[None],
        k_gain[None],
        scratch=[pltpu.VMEM((n_ctx, d_rows, 384), BF16)],
    )
    messages = sent_ahead(messages)
    w_near = jnp.concatenate([m[:, :384] for m in messages], axis=0)
    w_pair = jnp.concatenate([w_near, swap(w_near, "h")], axis=0)
    tokens_all = lax.all_gather(tokens[0], "y", axis=0, tiled=True)
    expert_rows = jnp.transpose(
        experts.reshape(d_rows, 2 * n_ctx, held, 3 * ff), (1, 0, 2, 3)
    ).reshape(2 * n_ctx, d_rows, held * 3 * ff)
    expert_rows = lax.all_to_all(after(expert_rows, w_near), ("c", "y"), 0, 0, tiled=True)
    expert_rows = expert_rows.reshape(2 * n_ctx * d_rows, held * 3 * ff)
    expert_other = swap(expert_rows, "h")
    expert_near = lax.all_gather(expert_rows, "x", axis=0, tiled=True)
    expert_far = lax.all_gather(expert_other, "x", axis=0, tiled=True)

    o_near = jnp.concatenate([m[:, 384:] for m in messages], axis=0)
    o_pair = jnp.concatenate([o_near, swap(o_near, "h")], axis=0)
    w_chunks = after(relative(w_pair, "x"), o_pair)
    w_own = jnp.concatenate(w_chunks, axis=0)
    u_own = call(
        route_kernel,
        [shape((n_ctx, rows, width + 128), BF16)],
        after(at, w_near),
        lengths,
        cotangent[0],
        expert_ids[0].T,
        router_gates[0].T,
        flops=2 * US,
    )[0]
    w_other = swap(after(w_own, expert_rows), "c")
    o_chunks = relative(after(o_pair, w_own), "x")

    weights, gains, into, raw, *parts = call(
        attend_kernel,
        [
            shape((width, 384), BF16),
            shape((2, width), F32),
            shape((seq, width), BF16),
            shape((seq, 256), F32),
            *[small] * 4,
        ],
        at,
        tokens_all,
        w_own,
        w_other,
        cosine,
        sine,
        scratch=[pltpu.VMEM((seq, 128), BF16)],
        flops=7 * US,
    )
    parts = sent_ahead(parts)
    o_own = jnp.concatenate(after(o_chunks, raw), axis=0)
    attn_low, mine, w_out = call(
        project_kernel,
        [shape((rows, 512), BF16), block, shape((width, 512), BF16)],
        after(at, expert_other),
        *parts,
        o_own,
        swap(o_own, "c"),
        flops=2 * US,
    )
    u_own = lax.all_to_all(after(u_own, attn_low), "y", 0, 0, tiled=True)
    u_own = u_own.reshape(seq, width + 128)
    resid, ffn_input = call(
        middle_kernel,
        [wide, block],
        mine,
        swap(mine, "l"),
        tokens[0],
        gains,
        flops=2 * US,
    )
    f_own = relative(ffn_input, "y")
    f_other = [swap(f, "c") for f in f_own]
    u_other = swap(after(u_own, *f_own), "c")

    def run_experts(f, u):
        return call(
            expert_kernel,
            [
                *[block] * 4,
                shape((seq, held * 3 * ff), BF16),
                shape((seq, width), BF16),
            ],
            at,
            *f,
            u,
            expert_near,
            expert_far,
            scratch=[pltpu.VMEM((seq, width), BF16)] * 2,
            flops=7 * US,
        )

    *part_other, g_other, out_other = run_experts(f_other, u_other)
    f_first = after(f_own, g_other)
    *part_own, g_own, out_own = run_experts(f_first, u_own)
    summed = [added(p, swap(q, "c")) for p, q in zip(part_own, part_other)]
    out_sum = added(out_own, swap(out_other, "c"))
    got = after(sent_ahead(summed), out_sum)
    mine = total_of(got)
    halves = shape((2, 2, n_ctx, 2, d_rows, 3 * ff), BF16)
    kept0, sent0, kept1, sent1 = call(
        expert_weights_kernel,
        [halves] * 4,
        after(at, summed),
        *f_own,
        *f_other,
        u_own,
        u_other,
        g_own,
        g_other,
        scratch=[
            pltpu.VMEM((width, 2 * seq), BF16),
            pltpu.VMEM((width, 2 * seq), BF16),
            pltpu.VMEM((width, 256), BF16),
        ],
        flops=10 * US,
    )
    resid_grad, out_grad, *attn_grads = call(
        middle_back_kernel,
        [wide, block, *[small] * 4],
        at,
        lengths,
        mine,
        swap(mine, "l"),
        resid,
        cotangent[0],
        gains,
        w_out,
        flops=3 * US,
    )
    attn_grads = sent_ahead(attn_grads)

    out_rows = lax.psum_scatter(after(out_sum, mine), "y", scatter_dimension=0, tiled=True)
    near = after([beside(sent0, True), beside(sent1, False)], attn_grads)
    kept = [added(kept0, near[0]), added(kept1, near[1])]
    far = [beside(k[1], e == 1) for e, k in enumerate(kept)]
    dw0, dw1, p0, p1, p2, p3 = call(
        attend_back_kernel,
        [shape((16, 2, d_rows, 896), BF16)] * 2 + [block] * 4,
        after(at, kept),
        *attn_grads,
        into,
        raw,
        weights,
        cosine,
        sine,
        out_grad,
        attn_low,
        scratch=[
            pltpu.VMEM((seq, 128), BF16),
            pltpu.VMEM((seq, width), BF16),
            pltpu.VMEM((width, 896), BF16),
        ],
        flops=US,
    )
    far = after(far, p0, out_rows)
    dw = added(dw0, swap(after(dw1, far), "c"))
    owned = lax.all_to_all(dw, ("x", "y"), 0, 0, tiled=True)
    owned = owned.reshape(4, n_ctx, 2, d_rows, 896).astype(F32)
    owned_into = jnp.sum(owned[..., :384], axis=0).reshape(n_ctx, 2, d_rows, 3, 128)
    owned_out = jnp.sum(owned[..., 384:], axis=(0, 1)).reshape(2, d_rows, 4, 128)
    owned = jnp.concatenate(
        [
            jnp.transpose(owned_into, (1, 3, 0, 2, 4)).reshape(2, -1, 128),
            jnp.transpose(owned_out, (0, 2, 1, 3)).reshape(2, -1, 128),
        ],
        axis=1,
    ).astype(BF16)
    owned_other = swap(lax.dynamic_index_in_dim(owned, 1 - at_h, 0, False), "h")
    owned = lax.dynamic_index_in_dim(owned, at_h, 0, False)
    mine = total_of(after(sent_ahead([p0, p1, p2, p3]), dw))
    tokens_grad = call(
        first_back_kernel,
        [wide],
        mine,
        swap(mine, "l"),
        resid_grad,
        tokens[0],
        gains,
        flops=2 * US,
    )[0]

    far = after(far, dw)
    sums = jnp.stack([added(k[0], f) for k, f in zip(kept, far)], axis=2)
    sums = added(sums[0], swap(sums[1], "h"))
    pieces = sent_ahead([sums[k] for k in range(n_ctx)])
    given = swap(jnp.stack([p[:, 1] for p in pieces]), "c")
    out_rows = added(out_rows, after(swap(out_rows, "l"), owned))
    *own_grads, expert_grads, ends = call(
        owner_kernel,
        [
            shape(w_query.shape, F32),
            shape(key_weight.shape, F32),
            shape(value_weight.shape, F32),
            shape(w_output.shape, F32),
            shape((d_rows, 3, num_experts, ff), F32),
            shape((2, 128), F32),
        ],
        after(at, out_rows),
        owned,
        owned_other,
        *[p[:, 0] for p in pieces],
        given,
        w_query,
        key_weight,
        value_weight,
        jnp.transpose(experts, (0, 2, 1, 3)),
        attn_gain[None],
        ffn_gain[None],
        scratch=[pltpu.VMEM((num_experts, d_rows, 3 * ff), BF16)],
        flops=4 * US,
    )
    positions = at_y * rows + jnp.arange(rows, dtype=jnp.int32)
    valid = (positions < lengths[0]).astype(F32)[:, None]
    mixed = (valid * (resid + out_rows.astype(F32))).astype(BF16)
    owner = ((at_h * 4 + at_x) * 2 + at_c) * n_ctx + at_y
    ends = ends + swap(ends, "l")
    pair = [lax.dynamic_slice(ends, (1, owner + k), (1, 1))[0] for k in (0, 64)]
    return (
        mixed[None],
        tokens_grad[None],
        ends[0, :d_rows],
        ends[0, d_rows : 2 * d_rows],
        *pair,
        *own_grads,
        jnp.transpose(expert_grads, (0, 2, 1, 3)),
    )


def solution(mesh):
    fine = Mesh(mesh.devices.reshape(2, 4, 2, 4, 2), ("h", "x", "c", "y", "l"))
    rows = P(("h", "x", "c"), "y", None)
    split = P(("h", "x", "c", "y"))
    heads = P(("h", "x", "c", "y"), "l", None)
    hidden = P(("h", "x", "c", "y"), None, None, "l")
    ins = (rows, rows, P(("h", "x", "c")), rows, rows)
    weights = (split, split, split, split, heads, heads, heads, heads, hidden)
    return jax.shard_map(
        local,
        mesh=fine,
        in_specs=ins + weights,
        out_specs=(rows, rows) + weights,
        check_vma=False,
    )
```

```python
import jax
import jax.numpy as jnp
import numpy as np
from jax import lax
from jax.experimental import pallas as pl
from jax.experimental.pallas import tpu as pltpu
from jax.sharding import Mesh, PartitionSpec as P

EPSILON = 1e-06
THETA_BASE = 1000000.0
NEG_FILL = -1e30
F32 = jnp.float32
BF16 = jnp.bfloat16
VMEM_LIMIT = 60 * 1024 * 1024
US = 1_100_000_000


def dot(a, b, ca=1, cb=0):
    return lax.dot_general(a, b, (((ca,), (cb,)), ((), ())), preferred_element_type=F32)


def inverse_rms(values):
    return lax.rsqrt(jnp.mean(values * values, axis=-1, keepdims=True) + EPSILON)


def norm_back(incoming, normed, inv_scale):
    return inv_scale * (incoming - normed * jnp.mean(incoming * normed, axis=-1, keepdims=True))


def rope_tables(seq, head_width):
    half = head_width // 2
    steps = np.tile(np.arange(half, dtype=np.float32), 4)
    frequency = np.float32(THETA_BASE) ** (-(steps * np.float32(2.0)) / np.float32(head_width))
    angles = np.arange(seq, dtype=np.float32)[:, None] * frequency[None, :]
    sign = np.where(np.arange(4 * half) % head_width < half, -1.0, 1.0).astype(np.float32)
    return jnp.asarray(np.cos(angles)), jnp.asarray(np.sin(angles) * sign)


def call(kernel, outs, *args, scratch=(), flops=0):
    smem = pl.BlockSpec(memory_space=pltpu.SMEM)
    vmem = pl.BlockSpec(memory_space=pltpu.VMEM)
    moved = sum(a.size * a.dtype.itemsize for a in args)
    moved += sum(o.size * o.dtype.itemsize for o in outs)
    return pl.pallas_call(
        kernel,
        out_shape=outs,
        in_specs=[smem if a.dtype == jnp.int32 and a.ndim == 1 else vmem for a in args],
        out_specs=[vmem] * len(outs),
        scratch_shapes=list(scratch),
        compiler_params=pltpu.CompilerParams(vmem_limit_bytes=VMEM_LIMIT),
        cost_estimate=pl.CostEstimate(flops=flops, bytes_accessed=moved, transcendentals=0),
    )(*args)


def shape(dims, dtype):
    return jax.ShapeDtypeStruct(dims, dtype)


def lanes(values):
    return lax.broadcasted_iota(jnp.int32, values.shape, len(values.shape) - 1)


def in_first(values):
    return lanes(values) < 64


def turned(values):
    return jnp.where(
        lanes(values) % 64 < 32, pltpu.roll(values, 96, 1), pltpu.roll(values, 32, 1)
    )


def doubled(values):
    return jnp.where(in_first(values), values, pltpu.roll(values, 64, 1))


def doubled_second(values):
    return jnp.where(in_first(values), pltpu.roll(values, 64, 1), values)


def head_mean(values):
    first = in_first(values)
    low = jnp.sum(jnp.where(first, values, 0.0), axis=1, keepdims=True)
    high = jnp.sum(jnp.where(first, 0.0, values), axis=1, keepdims=True)
    return jnp.where(first, low, high) * (1.0 / 64.0)


def head_only(values, g):
    keep = in_first(values) if g == 0 else lanes(values) >= 64
    return jnp.where(keep, values, jnp.zeros_like(values))


def head_gains(w_ref, n):
    column_q, column_k = w_ref[:, 258:259].astype(F32), w_ref[:, 259:260].astype(F32)
    row = lax.broadcasted_iota(jnp.int32, (w_ref.shape[0], 128), 0)
    lane = lanes(row) * n
    spread = jnp.where(row == lane, column_q, jnp.where(row == lane - 64 * n, column_k, 0.0))
    return jnp.sum(spread, axis=0, keepdims=True)


def row_of(w_ref, column):
    eye = lax.broadcasted_iota(jnp.int32, (128, 128), 0)
    eye = eye == lanes(eye)
    blocks = []
    for i in range(w_ref.shape[0] // 128):
        values = w_ref[i * 128 : (i + 1) * 128, column : column + 1].astype(F32)
        blocks.append(jnp.sum(jnp.where(eye, values, 0.0), axis=0, keepdims=True))
    return jnp.concatenate(blocks, axis=1)


def heads_of(raw, w_ref, n, cosine, sine):
    gains = head_gains(w_ref, n)
    gain_q, gain_k = doubled(gains), doubled_second(gains)
    q_raw, kv_raw = raw[:, :128], raw[:, 128:]
    q_inv = lax.rsqrt(head_mean(q_raw * q_raw) + EPSILON)
    k_inv = lax.rsqrt(head_mean(kv_raw * kv_raw) + EPSILON)
    q_hat, k_hat = q_raw * q_inv, kv_raw * k_inv
    q_turn, k_turn = q_hat * gain_q, k_hat * gain_k
    q = (q_turn * cosine + turned(q_turn) * sine).astype(BF16)
    k = (k_turn * cosine + turned(k_turn) * sine)
    k = doubled(k).astype(BF16)
    v = doubled_second(kv_raw).astype(BF16)
    return q, k, v, q_hat, k_hat, q_inv, k_inv, gain_q, gain_k


def probabilities(q, k, g, half):
    n = q.shape[0] // 2
    q, k = q[half * n : (half + 1) * n], k[: (half + 1) * n]
    scores = dot(head_only(q, g), k, 1, 1) * 0.125
    row = lax.broadcasted_iota(jnp.int32, scores.shape, 0) + half * n
    scores = jnp.where(lanes(scores) <= row, scores, NEG_FILL)
    exps = jnp.exp(scores - jnp.max(scores, axis=1, keepdims=True))
    return exps / jnp.sum(exps, axis=1, keepdims=True)


def column_of(ref):
    n = ref.shape[1]
    eye = lax.broadcasted_iota(jnp.int32, (n, n), 0)
    eye = eye == lanes(eye)
    return jnp.sum(jnp.where(eye, ref[...].astype(F32), 0.0), axis=1, keepdims=True)


def pack_kernel(wq, wk, wv, wo, one, two, qg, kg, m0, m1, m2, m3, held):
    n = wq.shape[0]
    lane = lax.broadcasted_iota(jnp.int32, (n, 128), 1)
    gains = jnp.where(lane == 0, column_of(one), jnp.where(lane == 1, column_of(two), 0.0))
    gains = jnp.where(lane == 2, qg[...].astype(F32), gains)
    gains = jnp.where(lane == 3, kg[...].astype(F32), gains).astype(BF16)
    q, k, v, o = (ref[...].astype(F32) for ref in (wq, wk, wv, wo))
    for j in range(4):
        held[j, :, 0:64] = q[:, 2 * j, :].astype(BF16)
        held[j, :, 64:128] = q[:, 2 * j + 1, :].astype(BF16)
        held[j, :, 128:192] = k[:, j, :].astype(BF16)
        held[j, :, 192:256] = v[:, j, :].astype(BF16)
        held[j, :, 256:384] = gains
    out = jnp.concatenate([o[:, i, :] for i in range(8)], axis=1).astype(BF16)
    at_y = lax.axis_index("y")
    for i, m in enumerate((m0, m1, m2, m3)):
        m[:, :384] = held[lax.rem(at_y + i, 4)]
        m[:, 384:] = out


def route_kernel(at, lengths, cot, ids, gates, copies):
    rows = cot.shape[0]
    row = lax.broadcasted_iota(jnp.int32, (rows, 1), 0) + at[0] * rows
    expert = lax.broadcasted_iota(jnp.int32, (rows, rows), 0)
    total = jnp.zeros((rows, rows), F32)
    for k in range(ids.shape[0]):
        total = total + jnp.where(ids[k : k + 1, :] == expert, gates[k : k + 1, :], 0.0)
    total = jnp.where(row < lengths[0], jnp.transpose(total), 0.0)
    high = total.astype(BF16).astype(F32)
    codes = (high + pltpu.roll(total - high, 16, 1)).astype(BF16)
    for i in range(copies.shape[0]):
        copies[i, :, :1024] = cot[...]
        copies[i, :, 1024:] = codes


def rows_in_order(at, arrived, out):
    n = arrived[0].shape[0] // 32
    for c, ref in enumerate(arrived):
        for i in range(32):
            y = lax.rem(at[0] + 4 - i % 4, 4)
            h = lax.rem(at[3] + i // 4 % 2, 2)
            x = lax.rem(at[4] + i // 8, 4)
            block = ((h * 4 + x) * 2 + lax.rem(at[1] + c, 2)) * 4 + y
            out[pl.ds(pl.multiple_of(block * n, n), n), :] = ref[i * n : (i + 1) * n, :]


def attend_kernel(
    at, tokens, wa, wb, cosine, sine, w, gains, into, raw, p0, p1, p2, p3, low
):
    n = wa.shape[0] // 32
    rows_in_order(at, (wa, wb), w)
    rows = p0.shape[0]
    gain_one = row_of(w, 256)
    gains[0:1, :] = gain_one
    gains[1:2, :] = row_of(w, 257)
    x = tokens[...].astype(F32)
    into[...] = (x * inverse_rms(x) * gain_one).astype(BF16)
    raw[...] = dot(into[...], w[:, :256])
    q, k, v = heads_of(raw[...], w, n, cosine[...], sine[...])[:3]
    n = q.shape[0] // 2
    for half in range(2):
        keys = slice(0, (half + 1) * n)
        out = [dot(probabilities(q, k, g, half).astype(BF16), v[keys]) for g in range(2)]
        low[half * n : (half + 1) * n, :] = jnp.where(in_first(out[0]), out[0], out[1]).astype(BF16)
    for k, part in enumerate((p0, p1, p2, p3)):
        start = pl.multiple_of(lax.rem(at[0] + k, 4) * rows, rows)
        part[...] = low[pl.ds(start, rows), :]


def spread_of(n):
    return 1.0 + lax.broadcasted_iota(jnp.int32, (n, 128), 0).astype(F32) * (1.0 / n)


def attend_back_kernel(
    at, g0, g1, g2, g3, into, raw, w, cosine, sine, og, a, dw0, dw1, p0, p1, p2, p3,
    grad, back, dw
):
    rows = g0.shape[0]
    for i, g in enumerate((g0, g1, g2, g3)):
        start = pl.multiple_of(lax.rem(at[0] + 4 - i, 4) * rows, rows)
        grad[pl.ds(start, rows), :] = g[...]
    n = dw0.shape[2]
    q, k, v, q_hat, k_hat, q_inv, k_inv, gain_q, gain_k = heads_of(
        raw[...], w, n, cosine[...], sine[...]
    )
    out_grad = grad[...]
    m = q.shape[0] // 2
    dq, dk, dv = [], [], []
    for half in range(2):
        rows_of, keys = slice(half * m, (half + 1) * m), slice(0, (half + 1) * m)
        dq_of, dk_of, dv_of = [], 0.0, 0.0
        for g in range(2):
            probs = probabilities(q, k, g, half)
            own = head_only(out_grad[rows_of], g)
            dv_of = dv_of + dot(probs.astype(BF16), own, 0, 0)
            probs_grad = dot(own, v[keys], 1, 1)
            delta = jnp.sum(probs * probs_grad, axis=1, keepdims=True)
            score_grad = (probs * (probs_grad - delta)).astype(BF16)
            dq_of.append(dot(score_grad, k[keys]))
            dk_of = dk_of + dot(score_grad, head_only(q[rows_of], g), 0, 0)
        dq.append(jnp.where(in_first(dq_of[0]), dq_of[0], dq_of[1]) * 0.125)
        dk.append(dk_of)
        dv.append(dv_of)
    dq = jnp.concatenate(dq, axis=0)
    dk = jnp.concatenate([dk[0] + dk[1][:m], dk[1][m:]], axis=0)
    dv = jnp.concatenate([dv[0] + dv[1][:m], dv[1][m:]], axis=0)
    dk = (dk + pltpu.roll(dk, 64, 1)) * 0.125
    dv = dv + pltpu.roll(dv, 64, 1)
    q_back = dq * cosine[...] - turned(dq) * sine[...]
    k_back = dk * cosine[...] - turned(dk) * sine[...]
    q_gain = jnp.sum(q_back * q_hat, axis=0, keepdims=True)
    k_gain = jnp.sum(k_back * k_hat, axis=0, keepdims=True)
    q_gain = q_gain + pltpu.roll(q_gain, 64, 1)
    k_gain = pltpu.roll(k_gain, 64, 1)
    q_scaled, k_scaled = q_back * gain_q, k_back * gain_k
    q_out = q_inv * (q_scaled - q_hat * head_mean(q_scaled * q_hat))
    k_out = k_inv * (k_scaled - k_hat * head_mean(k_scaled * k_hat))
    q_out = q_out.astype(BF16)
    kv_out = jnp.where(in_first(k_out), k_out, dv).astype(BF16)
    both = jnp.concatenate([q_out, kv_out], axis=1)
    back[...] = dot(both, w[:, :256], 1, 1).astype(BF16)
    for i, part in enumerate((p0, p1, p2, p3)):
        part[...] = back[pl.ds(pl.multiple_of(lax.rem(at[0] + i, 4) * rows, rows), rows), :]
    gains = (jnp.where(in_first(q_gain), q_gain, k_gain) * spread_of(n)).astype(BF16)
    dw[:, :256] = dot(into[...], both, 0, 0).astype(BF16)
    for i in range(64):
        dw[i * n : (i + 1) * n, 256:384] = gains
    dw[:, 384:] = dot(og[...], a[...], 0, 0).astype(BF16)
    for to in range(16):
        for h in range(2):
            block = (h * 4 + to // 4) * 8 + to % 4
            for r, out in enumerate((dw0, dw1)):
                start = pl.multiple_of((block + lax.rem(at[1] + r, 2) * 4) * n, n)
                out[to, h] = dw[pl.ds(start, n), :]


def project_kernel(at, p0, p1, p2, p3, wa, wb, a, part, w_out):
    rows_in_order(at, (wa, wb), w_out)
    total = 0.0
    for k, p in enumerate((p0, p1, p2, p3)):
        start = pl.multiple_of(lax.rem(at[0] + 4 - k, 4) * 128, 128)
        a[:, pl.ds(start, 128)] = p[...]
        total = total + dot(p[...], w_out[:, pl.ds(start, 128)], 1, 1)
    part[...] = total.astype(BF16)


def middle_kernel(mine, other, tokens, gains, resid, low):
    values = tokens[...].astype(F32) + (mine[...].astype(F32) + other[...].astype(F32))
    resid[...] = values
    low[...] = (values * inverse_rms(values) * gains[1:2, :]).astype(BF16)


def middle_back_kernel(
    at, lengths, mine, other, resid, cot, gains, w_out, resid_grad, low, p0, p1, p2, p3
):
    values = resid[...]
    row = lax.broadcasted_iota(jnp.int32, (values.shape[0], 1), 0) + at[0] * values.shape[0]
    upstream = jnp.where(row < lengths[0], cot[...].astype(F32), 0.0)
    inv = inverse_rms(values)
    incoming = (mine[...].astype(F32) + other[...].astype(F32)) * gains[1:2, :]
    total = upstream + norm_back(incoming, values * inv, inv)
    resid_grad[...] = total
    low[...] = total.astype(BF16)
    for k, p in enumerate((p0, p1, p2, p3)):
        start = pl.multiple_of(lax.rem(at[0] + k, 4) * 128, 128)
        p[...] = dot(low[...], w_out[:, pl.ds(start, 128)]).astype(BF16)


def first_back_kernel(mine, other, resid_grad, tokens, gains, out):
    x = tokens[...].astype(F32)
    inv = inverse_rms(x)
    incoming = (mine[...].astype(F32) + other[...].astype(F32)) * gains[0:1, :]
    out[...] = resid_grad[...] + norm_back(incoming, x * inv, inv)


def expert_kernel(at, f0, f1, f2, f3, u, wa, wb, p0, p1, p2, p3, grads, out, f, part):
    n = f0.shape[0]
    for k, block in enumerate((f0, f1, f2, f3)):
        f[pl.ds(pl.multiple_of(lax.rem(at[0] + k, 4) * n, n), n), :] = block[...]
    codes = u[:, 1024:].astype(F32)
    lane = lanes(codes)
    width = wa.shape[0]
    halves = [pl.ds(pl.multiple_of(lax.rem(at[3] + i, 2) * width, width), width) for i in range(2)]
    weights = list(zip((wa, wb), halves))
    for e in range(2):
        mine = (lane == at[2] + e) | (lane == at[2] + e + 16)
        gate = jnp.sum(jnp.where(mine, codes, 0.0), axis=1, keepdims=True)
        c = e * 768
        gate_up = sum(dot(f[:, d], w[:, c : c + 512]) for w, d in weights)
        hidden_grad = sum(dot(u[:, d], w[:, c + 512 : c + 768]) for w, d in weights) * gate
        gate_pre, up_pre = gate_up[:, :256], gate_up[:, 256:]
        sigma = jax.nn.sigmoid(gate_pre)
        activated = gate_pre * sigma
        slope = sigma + activated * (1.0 - sigma)
        grads[:, c : c + 256] = (hidden_grad * up_pre * slope).astype(BF16)
        grads[:, c + 256 : c + 512] = (hidden_grad * activated).astype(BF16)
        grads[:, c + 512 : c + 768] = (activated * up_pre * gate).astype(BF16)
    for w, d in weights:
        total = dot(grads[:, 0:512], w[:, 0:512], 1, 1)
        total = (total + dot(grads[:, 768:1280], w[:, 768:1280], 1, 1)).astype(BF16)
        part[:, d] = total
        total = dot(grads[:, 512:768], w[:, 512:768], 1, 1)
        total = total + dot(grads[:, 1280:1536], w[:, 1280:1536], 1, 1)
        out[:, d] = total.astype(BF16)
    for k, p in enumerate((p0, p1, p2, p3)):
        p[...] = part[pl.ds(pl.multiple_of(lax.rem(at[0] + k, 4) * n, n), n), :]


def expert_weights_kernel(at, *refs):
    blocks = (refs[0:4], refs[4:8])
    u0, u1, g0, g1, k0, s0, k1, s1, ft, ut, done = refs[8:]
    rows = u0.shape[0]
    n = k0.shape[4]
    for s, (f, u) in enumerate(zip(blocks, (u0, u1))):
        for k in range(4):
            start = pl.multiple_of(s * rows + lax.rem(at[0] + k, 4) * 128, 128)
            ft[:, pl.ds(start, 128)] = jnp.transpose(f[k][...])
        ut[:, s * rows : (s + 1) * rows] = jnp.transpose(u[:, :1024])

    def store(e, columns, into):
        keep, send = ((k0, s0), (k1, s1))[e]
        done[...] = into.astype(BF16)
        for i in range(64):
            r, h, y, c = i // 16, i // 8 % 2, i // 2 % 4, i % 2
            x = at[4] ^ ((0, 1, 3, 2), (0, 3, 1, 2))[e][r]
            h_to, c_to = lax.rem(at[3] + h, 2), lax.rem(at[1] + c, 2)
            y_to = lax.rem(at[0] + y, 4)
            start = pl.multiple_of((((h_to * 4 + x) * 2 + c_to) * 4 + y_to) * n, n)
            (keep if r < 2 else send)[r % 2, h, y, c, :, columns] = done[pl.ds(start, n), :]

    for e in range(2):

        @pl.loop(0, 2)
        def _(p, e=e):
            columns = pl.ds(pl.multiple_of(e * 768 + p * 256, 256), 256)
            into = dot(ft[:, :rows], g0[:, columns]) + dot(ft[:, rows:], g1[:, columns])
            store(e, pl.ds(pl.multiple_of(p * 256, 256), 256), into)

        columns = slice(e * 768 + 512, e * 768 + 768)
        down = dot(ut[:, :rows], g0[:, columns]) + dot(ut[:, rows:], g1[:, columns])
        store(e, slice(512, 768), down)


def owner_kernel(
    at, got, got_other, k0, k1, k2, k3, given, wq, wk, wv, we, one, two,
    dq, dk, dv, do, de, ends, held
):
    n = wq.shape[0]
    for c in range(2):
        for k, kept in enumerate((k0, k1, k2, k3)):
            y = lax.rem(at[0] + 4 - k, 4)
            first = (lax.rem(at[1] + c, 2) * 4 + y) * 2
            for e in range(2):
                held[first + e] = kept[e] if c == 0 else given[k, e]
    two_part = 0.0
    for x in range(3):
        for e in range(16):
            de[:, x, e, :] = held[e, :, x * 256 : (x + 1) * 256].astype(F32)
    for x in range(2):
        product = we[:, x].astype(F32) * de[:, x]
        two_part = two_part + jnp.sum(jnp.sum(product, axis=2), axis=1, keepdims=True)
    total = got[...].astype(F32) + got_other[...].astype(F32)
    block = lambda i: total[i * n : (i + 1) * n]
    rest = 0.0
    for j in range(4):
        for out, first, i in ((dq, 2 * j, j), (do, 2 * j, 12 + j)):
            out[:, first, :] = block(i)[:, 0:64]
            out[:, first + 1, :] = block(i)[:, 64:128]
        dk[:, j, :] = block(4 + j)[:, 0:64]
        dv[:, j, :] = block(4 + j)[:, 64:128]
        rest = rest + block(8 + j)
    one_part = 0.0
    for w, dw in ((wq, dq), (wk, dk), (wv, dv)):
        product = w[...].astype(F32) * dw[...]
        one_part = one_part + jnp.sum(jnp.sum(product, axis=2), axis=1, keepdims=True)
    gains = jnp.mean(rest / spread_of(n), axis=0, keepdims=True)
    row = lax.broadcasted_iota(jnp.int32, (n, 128), 0)
    lane = lanes(row)
    spread = jnp.where(lane == row, one_part / column_of(one), 0.0)
    spread = spread + jnp.where(lane == row + n, two_part / column_of(two), 0.0)
    ends[0:1, :] = jnp.sum(spread, axis=0, keepdims=True)
    ends[1:2, :] = gains


def swap(array, axis):
    return lax.ppermute(array, axis, [(0, 1), (1, 0)])


def from_ahead(array, axis, k):
    n = lax.axis_size(axis)
    return lax.ppermute(array, axis, [(i, (i - k) % n) for i in range(n)])


def to_ahead(array, axis, k):
    n = lax.axis_size(axis)
    return lax.ppermute(array, axis, [(i, (i + k) % n) for i in range(n)])


def ahead(axis, k):
    n = lax.axis_size(axis)
    return lax.rem(lax.axis_index(axis) + (k + n), n)


def after(value, *others):
    return lax.optimization_barrier((value, *others))[0]


def beside(array, odd):
    pairs = [(0, 3), (3, 0), (1, 2), (2, 1)] if odd else [(0, 1), (1, 0), (2, 3), (3, 2)]
    return lax.ppermute(array, "x", pairs)


def added(a, b):
    return (a.astype(F32) + b.astype(F32)).astype(BF16)


def relative(array, axis):
    return [array] + [from_ahead(array, axis, k) for k in range(1, lax.axis_size(axis))]


def sent_ahead(parts):
    return [to_ahead(p, "y", k) if k else p for k, p in enumerate(parts)]


def total_of(got):
    total = got[0].astype(F32)
    for g in got[1:]:
        total = total + g.astype(F32)
    return total.astype(BF16)


def local(
    tokens,
    cotangent,
    lengths,
    expert_ids,
    router_gates,
    attn_gain,
    ffn_gain,
    q_gain,
    k_gain,
    w_query,
    key_weight,
    value_weight,
    w_output,
    experts,
):
    rows, width = tokens.shape[1:]
    n_ctx = lax.axis_size("y")
    at_y, at_c = lax.axis_index("y"), lax.axis_index("c")
    at_h, at_x = lax.axis_index("h"), lax.axis_index("x")
    d_rows = w_query.shape[0]
    num_experts, _, ff = experts.shape[1:]
    held = num_experts // (n_ctx * 2)
    seq = rows * n_ctx
    apart = jnp.arange(4, dtype=jnp.int32) ^ at_x
    at = jnp.stack([at_y, at_c, (at_c * n_ctx + at_y) * held, at_h, at_x]).astype(jnp.int32)
    one_way = apart ^ (apart >> 1)
    other_way = (apart << 1) ^ ((apart >> 1) * 7)
    at = jnp.concatenate([at, one_way, other_way])
    cosine, sine = rope_tables(seq, w_query.shape[2])
    block = shape((rows, width), BF16)
    wide = shape((rows, width), F32)
    small = shape((rows, 128), BF16)

    messages = call(
        pack_kernel,
        [shape((d_rows, 896), BF16)] * 4,
        w_query,
        key_weight,
        value_weight,
        w_output,
        attn_gain[None],
        ffn_gain[None],
        q_gain[None],
        k_gain[None],
        scratch=[pltpu.VMEM((n_ctx, d_rows, 384), BF16)],
    )
    messages = sent_ahead(messages)
    w_near = jnp.concatenate([m[:, :384] for m in messages], axis=0)
    w_pair = jnp.concatenate([w_near, swap(w_near, "h")], axis=0)
    tokens_all = lax.all_gather(tokens[0], "y", axis=0, tiled=True)
    expert_rows = jnp.transpose(
        experts.reshape(d_rows, 2 * n_ctx, held, 3 * ff), (1, 0, 2, 3)
    ).reshape(2 * n_ctx, d_rows, held * 3 * ff)
    expert_rows = lax.all_to_all(after(expert_rows, w_near), ("c", "y"), 0, 0, tiled=True)
    expert_rows = expert_rows.reshape(2 * n_ctx * d_rows, held * 3 * ff)
    expert_other = swap(expert_rows, "h")
    expert_near = lax.all_gather(expert_rows, "x", axis=0, tiled=True)

    o_near = jnp.concatenate([m[:, 384:] for m in messages], axis=0)
    o_pair = jnp.concatenate([o_near, swap(o_near, "h")], axis=0)
    w_chunks = after(relative(w_pair, "x"), o_pair)
    w_own = jnp.concatenate(w_chunks, axis=0)
    u_own = call(
        route_kernel,
        [shape((n_ctx, rows, width + 128), BF16)],
        after(at, w_near),
        lengths,
        cotangent[0],
        expert_ids[0].T,
        router_gates[0].T,
        flops=2 * US,
    )[0]
    w_other = swap(after(w_own, expert_rows), "c")
    o_chunks = relative(after(o_pair, w_own), "x")

    weights, gains, into, raw, *parts = call(
        attend_kernel,
        [
            shape((width, 384), BF16),
            shape((2, width), F32),
            shape((seq, width), BF16),
            shape((seq, 256), F32),
            *[small] * 4,
        ],
        at,
        tokens_all,
        w_own,
        w_other,
        cosine,
        sine,
        scratch=[pltpu.VMEM((seq, 128), BF16)],
        flops=7 * US,
    )
    parts = sent_ahead(parts)
    expert_far = lax.all_gather(after(expert_other, parts[1]), "x", axis=0, tiled=True)
    o_own = jnp.concatenate(after(o_chunks, raw), axis=0)
    attn_low, mine, w_out = call(
        project_kernel,
        [shape((rows, 512), BF16), block, shape((width, 512), BF16)],
        after(at, expert_other),
        *parts,
        o_own,
        swap(o_own, "c"),
        flops=2 * US,
    )
    u_own = lax.all_to_all(after(u_own, attn_low), "y", 0, 0, tiled=True)
    u_own = u_own.reshape(seq, width + 128)
    resid, ffn_input = call(
        middle_kernel,
        [wide, block],
        mine,
        swap(mine, "l"),
        tokens[0],
        gains,
        flops=2 * US,
    )
    f_own = relative(ffn_input, "y")
    f_other = [swap(f, "c") for f in f_own]
    u_other = swap(after(u_own, *f_own), "c")

    def run_experts(f, u):
        return call(
            expert_kernel,
            [
                *[block] * 4,
                shape((seq, held * 3 * ff), BF16),
                shape((seq, width), BF16),
            ],
            at,
            *f,
            u,
            expert_near,
            expert_far,
            scratch=[pltpu.VMEM((seq, width), BF16)] * 2,
            flops=7 * US,
        )

    *part_other, g_other, out_other = run_experts(f_other, u_other)
    f_first = after(f_own, g_other)
    *part_own, g_own, out_own = run_experts(f_first, u_own)
    summed = [added(p, swap(q, "c")) for p, q in zip(part_own, part_other)]
    out_sum = added(out_own, swap(out_other, "c"))
    got = after(sent_ahead(summed), out_sum)
    mine = total_of(got)
    halves = shape((2, 2, n_ctx, 2, d_rows, 3 * ff), BF16)
    kept0, sent0, kept1, sent1 = call(
        expert_weights_kernel,
        [halves] * 4,
        after(at, summed),
        *f_own,
        *f_other,
        u_own,
        u_other,
        g_own,
        g_other,
        scratch=[
            pltpu.VMEM((width, 2 * seq), BF16),
            pltpu.VMEM((width, 2 * seq), BF16),
            pltpu.VMEM((width, 256), BF16),
        ],
        flops=10 * US,
    )
    resid_grad, out_grad, *attn_grads = call(
        middle_back_kernel,
        [wide, block, *[small] * 4],
        at,
        lengths,
        mine,
        swap(mine, "l"),
        resid,
        cotangent[0],
        gains,
        w_out,
        flops=3 * US,
    )
    attn_grads = sent_ahead(attn_grads)

    out_rows = lax.psum_scatter(after(out_sum, mine), "y", scatter_dimension=0, tiled=True)
    near = after([beside(sent0, True), beside(sent1, False)], attn_grads)
    kept = [added(kept0, near[0]), added(kept1, near[1])]
    far = [beside(k[1], e == 1) for e, k in enumerate(kept)]
    dw0, dw1, p0, p1, p2, p3 = call(
        attend_back_kernel,
        [shape((16, 2, d_rows, 896), BF16)] * 2 + [block] * 4,
        after(at, kept),
        *attn_grads,
        into,
        raw,
        weights,
        cosine,
        sine,
        out_grad,
        attn_low,
        scratch=[
            pltpu.VMEM((seq, 128), BF16),
            pltpu.VMEM((seq, width), BF16),
            pltpu.VMEM((width, 896), BF16),
        ],
        flops=US,
    )
    far = after(far, p0, out_rows)
    dw = added(dw0, swap(after(dw1, far), "c"))
    owned = lax.all_to_all(dw, ("x", "y"), 0, 0, tiled=True)
    owned = owned.reshape(4, n_ctx, 2, d_rows, 896).astype(F32)
    owned_into = jnp.sum(owned[..., :384], axis=0).reshape(n_ctx, 2, d_rows, 3, 128)
    owned_out = jnp.sum(owned[..., 384:], axis=(0, 1)).reshape(2, d_rows, 4, 128)
    owned = jnp.concatenate(
        [
            jnp.transpose(owned_into, (1, 3, 0, 2, 4)).reshape(2, -1, 128),
            jnp.transpose(owned_out, (0, 2, 1, 3)).reshape(2, -1, 128),
        ],
        axis=1,
    ).astype(BF16)
    owned_other = swap(lax.dynamic_index_in_dim(owned, 1 - at_h, 0, False), "h")
    owned = lax.dynamic_index_in_dim(owned, at_h, 0, False)
    mine = total_of(after(sent_ahead([p0, p1, p2, p3]), dw))
    tokens_grad = call(
        first_back_kernel,
        [wide],
        mine,
        swap(mine, "l"),
        resid_grad,
        tokens[0],
        gains,
        flops=2 * US,
    )[0]

    far = after(far, dw)
    sums = jnp.stack([added(k[0], f) for k, f in zip(kept, far)], axis=2)
    sums = added(sums[0], swap(sums[1], "h"))
    pieces = sent_ahead([sums[k] for k in range(n_ctx)])
    given = swap(jnp.stack([p[:, 1] for p in pieces]), "c")
    out_rows = added(out_rows, after(swap(out_rows, "l"), owned))
    *own_grads, expert_grads, ends = call(
        owner_kernel,
        [
            shape(w_query.shape, F32),
            shape(key_weight.shape, F32),
            shape(value_weight.shape, F32),
            shape(w_output.shape, F32),
            shape((d_rows, 3, num_experts, ff), F32),
            shape((2, 128), F32),
        ],
        after(at, out_rows),
        owned,
        owned_other,
        *[p[:, 0] for p in pieces],
        given,
        w_query,
        key_weight,
        value_weight,
        jnp.transpose(experts, (0, 2, 1, 3)),
        attn_gain[None],
        ffn_gain[None],
        scratch=[pltpu.VMEM((num_experts, d_rows, 3 * ff), BF16)],
        flops=4 * US,
    )
    positions = at_y * rows + jnp.arange(rows, dtype=jnp.int32)
    valid = (positions < lengths[0]).astype(F32)[:, None]
    mixed = (valid * (resid + out_rows.astype(F32))).astype(BF16)
    owner = ((at_h * 4 + at_x) * 2 + at_c) * n_ctx + at_y
    ends = ends + swap(ends, "l")
    pair = [lax.dynamic_slice(ends, (1, owner + k), (1, 1))[0] for k in (0, 64)]
    return (
        mixed[None],
        tokens_grad[None],
        ends[0, :d_rows],
        ends[0, d_rows : 2 * d_rows],
        *pair,
        *own_grads,
        jnp.transpose(expert_grads, (0, 2, 1, 3)),
    )


def solution(mesh):
    fine = Mesh(mesh.devices.reshape(2, 4, 2, 4, 2), ("h", "x", "c", "y", "l"))
    rows = P(("h", "x", "c"), "y", None)
    split = P(("h", "x", "c", "y"))
    heads = P(("h", "x", "c", "y"), "l", None)
    hidden = P(("h", "x", "c", "y"), None, None, "l")
    ins = (rows, rows, P(("h", "x", "c")), rows, rows)
    weights = (split, split, split, split, heads, heads, heads, heads, hidden)
    return jax.shard_map(
        local,
        mesh=fine,
        in_specs=ins + weights,
        out_specs=(rows, rows) + weights,
        check_vma=False,
    )
```
